32 devices in a mesh: dp: 8 (over z, x), mp: 4 (over y, core).
Axes of the slice: x: 2, y: 2, z: 4, core: 2. Of those that a mesh axis runs over, the one named last changes fastest.
Arguments:
- blocks: bfloat16 [32, 512, 512], P('dp'), may hold values from -6 to 6
- block_segment: int32 [32, 512], P('dp'), may hold values from 0 to 7, never falling along the last dimension, each value on 1 to 128 neighbouring positions
- upstream: bfloat16 [32, 512, 512], P('dp'), may hold values from -6 to 6
- attend_master: float32 [3, 512, 512], P(None, 'dp', 'mp'), may hold values from -0.25 to 0.25
- attend_first: float32 [3, 512, 512], P(None, 'dp', 'mp'), may hold values from -768 to 768
- attend_second: float32 [3, 512, 512], P(None, 'dp', 'mp'), may hold values from 10928.128 to 43696.13
- mixing_master: float32 [512, 512], P('mp', 'dp'), may hold values from -2 to 2
- mixing_first: float32 [512, 512], P('mp', 'dp'), may hold values from -96 to 96
- mixing_second: float32 [512, 512], P('mp', 'dp'), may hold values from 170.752 to 682.752
- expand_master: float32 [512, 2048], P('dp', 'mp'), may hold values from -0.25 to 0.25
- expand_first: float32 [512, 2048], P('dp', 'mp'), may hold values from -256 to 256
- expand_second: float32 [512, 2048], P('dp', 'mp'), may hold values from 1359.872 to 5455.872
- shrink_master: float32 [2048, 512], P('mp', 'dp'), may hold values from -0.125 to 0.125
- shrink_first: float32 [2048, 512], P('mp', 'dp'), may hold values from -512 to 512
- shrink_second: float32 [2048, 512], P('mp', 'dp'), may hold values from 5455.872 to 21839.871
- gains_master: float32 [2, 512], P(None, 'dp'), may hold values from 0.5 to 1.5
- gains_first: float32 [2, 512], P(None, 'dp'), may hold values from -896 to 896
- gains_second: float32 [2, 512], P(None, 'dp'), may hold values from 16384 to 65536
Outputs:
- result: bfloat16 [32, 512, 512], P('dp')
- blocks_grad: float32 [32, 512, 512], P('dp')
- attend_weight: float32 [3, 512, 512], P(None, 'dp', 'mp')
- attend_moment: float32 [3, 512, 512], P(None, 'dp', 'mp')
- attend_square: float32 [3, 512, 512], P(None, 'dp', 'mp')
- attend_copy: bfloat16 [3, 512, 512], P(None, 'dp', 'mp')
- mixing_weight: float32 [512, 512], P('mp', 'dp')
- mixing_moment: float32 [512, 512], P('mp', 'dp')
- mixing_square: float32 [512, 512], P('mp', 'dp')
- mixing_copy: bfloat16 [512, 512], P('mp', 'dp')
- expand_weight: float32 [512, 2048], P('dp', 'mp')
- expand_moment: float32 [512, 2048], P('dp', 'mp')
- expand_square: float32 [512, 2048], P('dp', 'mp')
- expand_copy: bfloat16 [512, 2048], P('dp', 'mp')
- shrink_weight: float32 [2048, 512], P('mp', 'dp')
- shrink_moment: float32 [2048, 512], P('mp', 'dp')
- shrink_square: float32 [2048, 512], P('mp', 'dp')
- shrink_copy: bfloat16 [2048, 512], P('mp', 'dp')
- gains_weight: float32 [2, 512], P(None, 'dp')
- gains_moment: float32 [2, 512], P(None, 'dp')
- gains_square: float32 [2, 512], P(None, 'dp')
- gains_copy: bfloat16 [2, 512], P(None, 'dp')
The draws below stay inside these ranges and needn't reach their ends.
Inputs may be any that keep to these rules, and one draw needn't show every extreme that they name: `block_segment`: in each row of 512 blocks the ids never fall and each id covers 1 to 128 consecutive blocks.
All inputs are finite; a program needn't handle non-finite values.
Results may differ from the reference program's by a relative error of at most 0.019.
Values may be sent and summed in bfloat16 or wider, within the bound.
No kernel may reach another device: no remote copies, remote signals or barrier semaphores. Data moves between devices by JAX's collectives and lax.ppermute only.
A program may use at most 128 MiB of HBM per device.

```python
import math
import jax
import jax.numpy as jnp
import numpy as np
from jax import lax

D = 512
H = 8
HD = 64
FF = 2048
SEQ = 512
SEGS = 8
STEP = 5
ROWS_DEV = 4
ROWS = 32
TOKENS = 16384
N_MP = 4


def with_spikes(result, rng, source, target, parts, factor):
    owner, partner = [(jnp.arange(result.shape[axis_at]) // (result.shape[axis_at] // parts)).reshape([-1 if axis == axis_at else 1 for axis in range(result.ndim)]) for axis_at in (source, target)]
    chosen = jax.random.permutation(rng, parts)[partner]
    strong = (owner == chosen) | (owner == (partner + parts // 2) % parts)
    return jnp.where(strong, factor * result, result)


def block_levels(own_key, shape, cuts, low, top_value):
    def one(axis_at, shards_of):
        draws = jax.random.uniform(jax.random.fold_in(jax.random.fold_in(own_key, 6), axis_at), (shards_of,), jnp.float32, low / len(cuts), top_value / len(cuts))
        return jnp.repeat(jnp.exp(draws), shape[axis_at] // shards_of).reshape((-1,) + (1,) * (len(shape) - axis_at - 1))

    loudness = one(*cuts[0])
    for cut in cuts[1:]:
        loudness = loudness * one(*cut)
    return loudness


def split_up(number_of, total, bound, lean):
    loads = [(1 << 20) // math.isqrt(standing ** lean) + 1 for standing in range(2, number_of + 1)]
    surplus, given = total - bound - (number_of - 1), [1] * (number_of - 1)
    while surplus > 0:
        movable = [i for i in range(number_of - 1) if given[i] < bound]
        whole, left = sum([loads[i] for i in movable]), surplus
        for i in movable:
            addition = min(bound - given[i], max(1, left * loads[i] // whole), surplus)
            given[i] = given[i] + addition
            surplus = surplus - addition
    return np.array([bound] + given)


def uneven(rng, amount, total, bound, skew):
    if amount == 2:
        one = jax.random.randint(rng, (), max(1, total - bound), min(bound, total - 1) + 1)
        return jnp.stack([one, total - one])
    tallies = jnp.asarray(split_up(amount, total, bound, skew), jnp.int32)
    couples = (amount - 1) // 2
    source_of, receiver = tallies[1:1 + 2 * couples:2], tallies[2:2 + 2 * couples:2]
    margin = jnp.minimum(source_of - 1, bound - receiver)
    shifted = jax.random.randint(jax.random.fold_in(rng, 1), (couples,), 0, 1 << 20) % (margin + 1)
    tallies = tallies.at[1:1 + 2 * couples:2].set(source_of - shifted).at[2:2 + 2 * couples:2].set(receiver + shifted)
    return tallies[jax.random.permutation(jax.random.fold_in(rng, 2), amount)]


def scatter_about(own_key, dims, spread, reach, shards=(), held_as=jnp.bfloat16):
    array = spread * jax.random.normal(own_key, dims, jnp.float32)
    if shards:
        array = array * block_levels(own_key, dims, shards, -0.22, 0.18)
    return jnp.clip(array, -reach, reach).astype(held_as)


def bell_draw_with(own_key, dims, deviation, most, shards, heavy, held_as=jnp.bfloat16):
    drawn = deviation * jax.random.normal(own_key, dims, jnp.float32)
    if shards:
        drawn = drawn * block_levels(own_key, dims, shards, -0.22, 0.18)
    return jnp.clip(with_spikes(drawn, jax.random.fold_in(own_key, 3), *heavy), -most, most).astype(held_as)


def setup_inputs(seed: int = 0) -> dict:
    key_list = jax.random.split(jax.random.key(seed), 19)
    blocks = scatter_about(key_list[0], (ROWS, SEQ, D), 1.0, 6.0, ((0, 8),))
    block_segment = jax.vmap(lambda own: jnp.searchsorted(jnp.cumsum(uneven(own, SEGS, SEQ, SEQ // 4, 1)), jnp.arange(SEQ), side="right"))(jax.random.split(key_list[1], ROWS)).reshape((ROWS, SEQ)).astype(jnp.int32)
    upstream = bell_draw_with(key_list[2], (ROWS, SEQ, D), 1.0, 6.0, ((0, 8),), (0, 2, 8, 2.0))
    attend_master = scatter_about(key_list[3], (3, D, D), D ** -0.5, 0.25, ((1, 8), (2, 4)), jnp.float32)
    attend_first = scatter_about(key_list[4], (3, D, D), (TOKENS ** 0.5), 768.0, ((1, 8), (2, 4)), jnp.float32)
    attend_second = jnp.clip(jnp.exp(math.log(43696.13) - 1.3859195 * jax.random.uniform(key_list[5], (3, D, D), jnp.float32) ** block_levels(key_list[5], (3, D, D), ((1, 8), (2, 4)), -0.2, 0.2)), 10928.128, 43696.13)
    mixing_master = scatter_about(key_list[6], (D, D), (D * SEGS // SEQ) ** -0.5, 2.0, ((0, 4), (1, 8)), jnp.float32)
    mixing_first = scatter_about(key_list[7], (D, D), ((TOKENS * SEGS // SEQ) ** 0.5), 96.0, ((0, 4), (1, 8)), jnp.float32)
    mixing_second = jnp.clip(jnp.exp(math.log(682.752) - 1.3859195 * jax.random.uniform(key_list[8], (D, D), jnp.float32) ** block_levels(key_list[8], (D, D), ((0, 4), (1, 8)), -0.2, 0.2)), 170.752, 682.752)
    expand_master = scatter_about(key_list[9], (D, FF), D ** -0.5, 0.25, ((0, 8), (1, 4)), jnp.float32)
    expand_first = scatter_about(key_list[10], (D, FF), (0.35 * TOKENS ** 0.5), 256.0, ((0, 8), (1, 4)), jnp.float32)
    expand_second = jnp.clip(jnp.exp(math.log(5455.872) - 1.3893019 * jax.random.uniform(key_list[11], (D, FF), jnp.float32) ** block_levels(key_list[11], (D, FF), ((0, 8), (1, 4)), -0.2, 0.2)), 1359.872, 5455.872)
    shrink_master = scatter_about(key_list[12], (FF, D), FF ** -0.5, 0.125, ((0, 4), (1, 8)), jnp.float32)
    shrink_first = scatter_about(key_list[13], (FF, D), (0.7 * TOKENS ** 0.5), 512.0, ((0, 4), (1, 8)), jnp.float32)
    shrink_second = jnp.clip(jnp.exp(math.log(21839.871) - 1.3870448 * jax.random.uniform(key_list[14], (FF, D), jnp.float32) ** block_levels(key_list[14], (FF, D), ((0, 4), (1, 8)), -0.2, 0.2)), 5455.872, 21839.871)
    gains_master = jnp.clip(1.0 + 0.1 * jax.random.normal(key_list[15], (2, D), jnp.float32), 0.5, 1.5)
    gains_first = scatter_about(key_list[16], (2, D), (1.2 * TOKENS ** 0.5), 896.0, ((1, 8),), jnp.float32)
    gains_second = jnp.clip(jnp.exp(math.log(65536.0) - 1.3862944 * jax.random.uniform(key_list[17], (2, D), jnp.float32) ** block_levels(key_list[17], (2, D), ((1, 8),), -0.2, 0.2)), 16384.0, 65536.0)
    return {"blocks": blocks, "block_segment": block_segment, "upstream": upstream, "attend_master": attend_master, "attend_first": attend_first, "attend_second": attend_second, "mixing_master": mixing_master, "mixing_first": mixing_first, "mixing_second": mixing_second, "expand_master": expand_master, "expand_first": expand_first, "expand_second": expand_second, "shrink_master": shrink_master, "shrink_first": shrink_first, "shrink_second": shrink_second, "gains_master": gains_master, "gains_first": gains_first, "gains_second": gains_second}


@jax.custom_vjp
def low(v):
    return lax.optimization_barrier(v.astype(jnp.bfloat16)).astype(jnp.float32)

@jax.custom_vjp
def low_back(v):
    return v

def low_keep(v):
    return (low(v), None)

def low_pass(kept, grad):
    return (grad,)

def back_keep(v):
    return (v, None)

def back_low(kept, grad):
    return (low(grad),)
low.defvjp(low_keep, low_pass)
low_back.defvjp(back_keep, back_low)
epsilon = 1e-06
highest = lax.Precision.HIGHEST
step_rates = (0.05, 0.3, 0.05, 0.025, 0.25)
decay_rates = (0.1, 0.1, 0.1, 0.1, 0.0)
gelu_coef = 0.79788456
cubic_coef = 0.044715

def gelu_tanh(values):
    return 0.5 * values * (1.0 + jnp.tanh(gelu_coef * (values + cubic_coef * values * values * values)))

def rms_scale(values):
    return lax.rsqrt(lax.optimization_barrier(jnp.mean(values * values, axis=-1, keepdims=True)) + epsilon)

def group_forward(inputs, segment, attend, mixing, expand, shrink, gain_rows):
    row_count = inputs.shape[0]
    tokens = row_count * SEQ
    states = inputs.reshape(tokens, D)
    normed = low(states * rms_scale(states) * gain_rows[0])
    project = jnp.einsum('td,cdk->ctk', normed, attend, precision=highest)
    project = low(low_back(project)).reshape(3, row_count, SEQ, H, HD)
    scores = jnp.einsum('rqhe,rkhe->rhqk', project[0], project[1], precision=highest) * HD ** (-0.5)
    scores = low_back(scores)
    allowed = (segment[:, :, None] == segment[:, None, :])[:, None]
    scores = jnp.where(allowed, scores, -1e+30)
    weights = low(jax.nn.softmax(scores, axis=-1))
    mixed = jnp.einsum('rhqk,rkhe->rqhe', weights, project[2], precision=highest)
    mixed = low(low_back(mixed)).reshape(tokens, N_MP, D // N_MP)
    terms = jnp.einsum('tgk,gkd->tgd', mixed, mixing.reshape(N_MP, D // N_MP, D), precision=highest)
    attended = low_back(lax.optimization_barrier(jnp.sum(low(terms), axis=1)))
    hidden = states + attended
    normed_two = low(hidden * rms_scale(hidden) * gain_rows[1])
    inner = low_back(jnp.dot(normed_two, expand, precision=highest))
    active = low(gelu_tanh(inner)).reshape(tokens, N_MP, FF // N_MP)
    terms_two = jnp.einsum('tgk,gkd->tgd', active, shrink.reshape(N_MP, FF // N_MP, D), precision=highest)
    return (hidden + lax.optimization_barrier(jnp.sum(low(terms_two), axis=1))).reshape(row_count, SEQ, D)

def adam_step(master, moment, second, gradient, step_rate, weight_decay):
    moment_new = 0.5 * moment + 0.5 * gradient
    second_new = 0.6 * second + 0.4 * gradient * gradient
    fix_first = 1.0 - 0.5 ** STEP
    fix_second = 1.0 - 0.6 ** STEP
    update = moment_new / fix_first / (jnp.sqrt(second_new / fix_second) + 1e-08)
    master_new = master - step_rate * (update + weight_decay * master)
    return (master_new, moment_new, second_new, master_new.astype(jnp.bfloat16))

def reference(blocks, block_segment, upstream, attend_master, attend_first, attend_second, mixing_master, mixing_first, mixing_second, expand_master, expand_first, expand_second, shrink_master, shrink_first, shrink_second, gains_master, gains_first, gains_second):
    masters = (attend_master, mixing_master, expand_master, shrink_master, gains_master)

    def whole(states, weight_set):
        attend = low(weight_set[0])
        mixing = low(weight_set[1])
        expand = low(weight_set[2])
        shrink = low(weight_set[3])
        gain_rows = low(weight_set[4])
        grouped = states.reshape(-1, ROWS_DEV, SEQ, D)
        segments = block_segment.reshape(-1, ROWS_DEV, SEQ)

        def one_group(paired):
            return group_forward(paired[0], paired[1], attend, mixing, expand, shrink, gain_rows)
        outputs = lax.map(jax.checkpoint(one_group), (grouped, segments))
        return outputs.reshape(states.shape)
    outputs, pullback = jax.vjp(whole, blocks.astype(jnp.float32), masters)
    blocks_grad, gradients = pullback(upstream.astype(jnp.float32))
    moments = (attend_first, mixing_first, expand_first, shrink_first, gains_first)
    seconds = (attend_second, mixing_second, expand_second, shrink_second, gains_second)
    updated = []
    for index_kind in range(5):
        updated.extend(adam_step(masters[index_kind], moments[index_kind], seconds[index_kind], gradients[index_kind], step_rates[index_kind], decay_rates[index_kind]))
    return (outputs.astype(jnp.bfloat16), blocks_grad, updated[0], updated[1], updated[2], updated[3], updated[4], updated[5], updated[6], updated[7], updated[8], updated[9], updated[10], updated[11], updated[12], updated[13], updated[14], updated[15], updated[16], updated[17], updated[18], updated[19])
```

```python
import functools

import jax
import jax.numpy as jnp
from jax import lax
from jax.experimental import pallas as pl
from jax.experimental.pallas import tpu as pltpu
from jax.sharding import PartitionSpec as P

HD = 64
STEP = 5
TILE = 128
EPS = 1e-06
GELU = 0.79788456
CUBIC = 0.044715
BF = jnp.bfloat16
F32 = jnp.float32
VMEM_LIMIT = 56 * 1024 * 1024


def nn(a, b):
    return lax.dot_general(a, b, (((1,), (0,)), ((), ())), preferred_element_type=F32)


def nt(a, b):
    return lax.dot_general(a, b, (((1,), (1,)), ((), ())), preferred_element_type=F32)


def tn(a, b):
    return lax.dot_general(a, b, (((0,), (0,)), ((), ())), preferred_element_type=F32)


def root_scale(values):
    return lax.rsqrt(jnp.mean(values * values, axis=-1, keepdims=True) + EPS)


def call(body, outs, ins, scratch=(), prefetch=(), flops=0, moved=0, trans=0, maps=None, grid=(1,)):
    def whole(shape):
        return pl.BlockSpec(shape, lambda i, *s, n=len(shape): (0,) * n)

    maps = maps or {}
    in_specs = [maps.get(k) or whole(a.shape) for k, a in enumerate(ins)]
    out_specs = [maps.get(("out", k)) or whole(o.shape) for k, o in enumerate(outs)]
    return pl.pallas_call(
        body,
        out_shape=outs,
        grid_spec=pltpu.PrefetchScalarGridSpec(
            num_scalar_prefetch=len(prefetch),
            grid=grid,
            in_specs=in_specs,
            out_specs=out_specs,
            scratch_shapes=list(scratch),
        ),
        compiler_params=pltpu.CompilerParams(vmem_limit_bytes=VMEM_LIMIT),
        cost_estimate=pl.CostEstimate(flops=flops, bytes_accessed=moved, transcendentals=trans),
    )(*prefetch, *ins)


def pieces_of(refs, count, rows):
    half = count // 2
    for core in range(2):
        own, over_x, over_y, far_low, far_high = refs[5 * core : 5 * core + 5]
        yield core, 0, 0, count, own
        yield core, 1, 0, count, over_x
        yield 2 + core, 0, 0, count, over_y
        yield 2 + core, 1, 0, half, far_low
        yield 2 + core, 1, half, count - half, far_high


def place(refs, z, x, count, rows, store):
    for group, x_off, first, blocks, ref in pieces_of(refs, count, rows):
        x_at = lax.rem(x + x_off, 2)
        for k in range(blocks):
            z_at = lax.rem(z + (count - (first + k)), count)
            at = pl.multiple_of((z_at * 2 + x_at) * rows, rows)
            store(group, at, ref[k * rows : (k + 1) * rows, :])


def in_relative_rows(source, target, z, x, count, rows):
    half = count // 2
    for k in range(count):
        z_at = lax.rem(z + k, count)
        for x_off in range(2):
            x_at = lax.rem(x + x_off, 2)
            at = pl.multiple_of((z_at * 2 + x_at) * rows, rows)
            to = ((k // half) * 2 + x_off) * half * rows + (k % half) * rows
            target[to : to + rows, :] = source[pl.ds(at, rows), :]


def attention_kernel(count, rows, place_ref, x_ref, seg_col, seg_row, *refs):
    pieces, (h_ref, qkvo, p_ref, w_ref) = refs[:10], refs[10:]
    z, x = place_ref[0], place_ref[1]

    def store(group, at, block):
        for part in range(4):
            w_ref[pl.ds(at, rows), part * 512 + group * 128 : part * 512 + group * 128 + 128] = block[
                :, part * 128 : part * 128 + 128
            ]

    place(pieces, z, x, count, rows, store)
    states = x_ref[0].astype(F32)
    unit = (states * root_scale(states)).astype(BF)
    for part in range(3):
        qkvo[:, part * 512 : part * 512 + 512] = nn(unit, w_ref[:, part * 512 : part * 512 + 512]).astype(BF)
    lane = lax.broadcasted_iota(jnp.int32, (1, 128), 1)
    sides = [jnp.where(lane // HD == j, HD**-0.5, 0.0).astype(BF) for j in range(2)]
    tiles = qkvo.shape[0] // TILE
    for i in range(tiles):
        low = max(0, i - 1) * TILE
        wide = min(tiles, i + 2) * TILE - low
        mask = seg_col[i * TILE : (i + 1) * TILE, :] == seg_row[:, low : low + wide]
        for m in range(4):
            q = qkvo[i * TILE : (i + 1) * TILE, m * 128 : m * 128 + 128]
            k = qkvo[low : low + wide, 512 + m * 128 : 512 + m * 128 + 128]
            v = qkvo[low : low + wide, 1024 + m * 128 : 1024 + m * 128 + 128]
            o = []
            for j in range(2):
                s = jnp.where(mask, nt(q * sides[j], k), -1e30)
                e = jnp.exp(s - jnp.max(s, axis=-1, keepdims=True))
                p = (e * (1.0 / jnp.sum(e, axis=-1, keepdims=True))).astype(BF)
                p_ref[m * 2 + j, i, :, :wide] = p
                o.append(nn(p, v))
            qkvo[i * TILE : (i + 1) * TILE, 1536 + m * 128 : 1536 + m * 128 + 128] = jnp.where(
                lane < HD, o[0], o[1]
            ).astype(BF)
    h_ref[...] = states + nt(qkvo[:, 1536:2048], w_ref[:, 1536:2048])


def feed_kernel(count, rows, place_ref, h_ref, c_ref, *refs):
    pieces = refs[:10]
    res_ref, dh_ref, gain_ref, own_ref, sib_ref, w_e, w_s, u_flat, c_flat, u_rel, c_rel, acc_f, acc_d = refs[10:]
    z, x = place_ref[0], place_ref[1]
    cols = w_e.shape[2]

    def store(group, at, block):
        w_e[group, pl.ds(at, rows), :] = block[:, :cols]
        w_s[group, pl.ds(at, rows), :] = block[:, cols:]

    place(pieces, z, x, count, rows, store)
    h = h_ref[...]
    scale = root_scale(h)
    unit = h * scale
    low = unit.astype(BF)
    back = c_ref[0]
    u_flat[...] = low.T
    c_flat[...] = back.T
    in_relative_rows(u_flat, u_rel, z, x, count, rows)
    in_relative_rows(c_flat, c_rel, z, x, count, rows)
    for m in range(4):
        target = (own_ref, sib_ref)[m % 2]
        inner = nn(low, w_e[m])
        bent = jnp.tanh(GELU * (inner + CUBIC * inner * inner * inner))
        active = (0.5 * inner * (1.0 + bent)).astype(BF)
        slope = 0.5 * (1.0 + bent) + 0.5 * inner * (1.0 - bent * bent) * GELU * (
            1.0 + 3.0 * CUBIC * inner * inner
        )
        grad = (nn(back, w_s[m]) * slope).astype(BF)
        forward = nt(active, w_s[m])
        inward = nt(grad, w_e[m])
        if m == 0:
            acc_f[...] = forward
            acc_d[...] = inward
        else:
            acc_f[...] += forward
            acc_d[...] += inward
        shape = (2, 2, target.shape[3], cols)
        target[:, m // 2, :, :, :cols] = nn(u_rel[...], grad).astype(BF).reshape(shape)
        target[:, m // 2, :, :, cols:] = nn(c_rel[...], active).astype(BF).reshape(shape)
    res_ref[...] = (h + acc_f[...]).astype(BF)
    pushed = acc_d[...]
    both = pushed * unit
    gain_ref[...] = jnp.broadcast_to(jnp.sum(both, axis=0, keepdims=True), gain_ref.shape)
    dh_ref[...] = back.astype(F32) + scale * (pushed - unit * jnp.mean(both, axis=-1, keepdims=True))


def attention_back_kernel(count, rows, place_ref, dh_ref, x_ref, qkvo, p_ref, w_ref, *refs):
    bg_ref, bgl_ref, gain_ref, own_ref, sib_ref, flat, rel, do_ref, dqkv, acc_k, acc_v = refs
    z, x = place_ref[0], place_ref[1]
    low = dh_ref[...].astype(BF)
    do_ref[...] = nn(low, w_ref[:, 1536:2048]).astype(BF)
    flat[...] = low.T
    in_relative_rows(flat, rel, z, x, count, rows)
    shape = (2, 2, own_ref.shape[3], 128)

    def put(part, value):
        for m in range(4):
            target = (own_ref, sib_ref)[m % 2]
            target[:, m // 2, :, :, part * 128 : part * 128 + 128] = (
                value[:, m * 128 : m * 128 + 128].astype(BF).reshape(shape)
            )

    put(3, nn(rel[...], qkvo[:, 1536:2048]))
    lane = lax.broadcasted_iota(jnp.int32, (1, 128), 1)
    sides = [(lane // HD == j).astype(BF) for j in range(2)]
    halves = [(lane // HD == j).astype(F32) for j in range(2)]
    tiles = dqkv.shape[0] // TILE
    for m in range(4):
        acc_k[...] = jnp.zeros_like(acc_k)
        acc_v[...] = jnp.zeros_like(acc_v)
        for i in range(tiles):
            first = max(0, i - 1) * TILE
            wide = min(tiles, i + 2) * TILE - first
            here = slice(i * TILE, (i + 1) * TILE)
            there = slice(first, first + wide)
            at = slice(m * 128, m * 128 + 128)
            q = qkvo[here, at]
            k = qkvo[there, 512 + m * 128 : 512 + m * 128 + 128]
            v = qkvo[there, 1024 + m * 128 : 1024 + m * 128 + 128]
            do = do_ref[here, at]
            inside = do.astype(F32) * qkvo[here, 1536 + m * 128 : 1536 + m * 128 + 128].astype(F32)
            dq = 0.0
            for j in range(2):
                p = p_ref[m * 2 + j, i, :, :wide]
                do_j = do * sides[j]
                delta = jnp.sum(inside * halves[j], axis=-1, keepdims=True)
                ds = (p.astype(F32) * (nt(do_j, v) - delta)).astype(BF)
                dq = dq + nn(ds, k * sides[j])
                acc_k[there, :] += tn(ds, q * sides[j])
                acc_v[there, :] += tn(p, do_j)
            dqkv[here, at] = (dq * HD**-0.5).astype(BF)
        dqkv[:, 512 + m * 128 : 512 + m * 128 + 128] = (acc_k[...] * HD**-0.5).astype(BF)
        dqkv[:, 1024 + m * 128 : 1024 + m * 128 + 128] = acc_v[...].astype(BF)
    states = x_ref[0].astype(F32)
    scale = root_scale(states)
    unit = states * scale
    flat[...] = unit.astype(BF).T
    in_relative_rows(flat, rel, z, x, count, rows)
    for part in range(3):
        put(part, nn(rel[...], dqkv[:, part * 512 : part * 512 + 512]))
    pushed = nt(dqkv[...], w_ref[:, :1536])
    both = pushed * unit
    gain_ref[...] = jnp.broadcast_to(jnp.sum(both, axis=0, keepdims=True), gain_ref.shape)
    out = dh_ref[...] + scale * (pushed - unit * jnp.mean(both, axis=-1, keepdims=True))
    bg_ref[...] = out
    bgl_ref[...] = out.astype(BF)


def adam(master, moment, second, gradient, rate, decay):
    moment_new = 0.5 * moment + 0.5 * gradient
    second_new = 0.6 * second + 0.4 * gradient * gradient
    update = moment_new / (1.0 - 0.5**STEP) / (jnp.sqrt(second_new / (1.0 - 0.6**STEP)) + 1e-08)
    return master - rate * (update + decay * master), moment_new, second_new


def adam_into(outs, state, gradient, rate, decay):
    master, moment, second = adam(*state, gradient, rate, decay)
    outs[0][...] = master
    outs[1][...] = moment
    outs[2][...] = second
    outs[3][...] = master.astype(BF)


def total(refs):
    whole = refs[0][...].astype(F32)
    for ref in refs[1:]:
        whole = whole + ref[...].astype(F32)
    return whole


def feed_update_kernel(count, *refs):
    terms, gain, state, outs = refs[:count], refs[count], refs[count + 1 : count + 7], refs[count + 7 :]
    grad = total(terms)
    cols = state[0].shape[1]
    scaled = grad[:, :cols] * gain[:, 1:2].astype(BF).astype(F32)
    adam_into(outs[:4], [r[...] for r in state[:3]], scaled, 0.05, 0.1)
    adam_into(outs[4:], [r[...] for r in state[3:]], grad[:, cols:], 0.025, 0.1)


def attention_update_kernel(count, *refs):
    terms, gain, state, outs = refs[:count], refs[count], refs[count + 1 : count + 7], refs[count + 7 :]
    grad = total(terms)
    scale = gain[:, 0:1].astype(BF).astype(F32)
    for part in range(3):
        master, moment, second = adam(
            *[r[part] for r in state[:3]], grad[:, part * 128 : part * 128 + 128] * scale, 0.05, 0.1
        )
        outs[0][part] = master
        outs[1][part] = moment
        outs[2][part] = second
        outs[3][part] = master.astype(BF)
    adam_into(outs[4:], [r[...] for r in state[3:]], grad[:, 384:512], 0.3, 0.1)


def prepare_kernel(gain, attend, mixing, expand, shrink, first, second):
    gain_one = gain[:, 0:1].astype(BF).astype(F32)
    gain_two = gain[:, 1:2].astype(BF).astype(F32)
    cols = expand.shape[1]
    for part in range(3):
        first[:, part * 128 : part * 128 + 128] = (attend[part].astype(BF).astype(F32) * gain_one).astype(BF)
    first[:, 384:512] = mixing[...].astype(BF)
    second[:, :cols] = (expand[...].astype(BF).astype(F32) * gain_two).astype(BF)
    second[:, cols:] = shrink[...].astype(BF)


def rows_kernel(place_ref, own, sib, across, far, out_ref):
    step = pl.program_id(0)
    for k, ref in enumerate((own, sib, across, far)):

        @pl.when(step == k)
        def _(ref=ref):
            out_ref[0] = ref[...].astype(out_ref.dtype)


def struct(shape, dtype):
    return jax.ShapeDtypeStruct(shape, dtype)


def over_x(value):
    n = lax.axis_size("dp")
    return lax.ppermute(value, "dp", [(i, i ^ 1) for i in range(n)])


def over_z(value, k):
    n = lax.axis_size("dp")
    return lax.ppermute(value, "dp", [(i, (i + 2 * k) % n) for i in range(n)])


def over_y(value):
    return lax.ppermute(value, "mp", [(i, i ^ 2) for i in range(4)])


def over_core(value):
    return lax.ppermute(value, "mp", [(i, i ^ 1) for i in range(4)])


def gather_z(block, count):
    return jnp.concatenate([block] + [over_z(block, k) for k in range(1, count)], axis=0)


def gather_plane(column):
    half = column.shape[0] // 2
    near_x, near_y = over_x(column), over_y(column)
    far_low, far_high = over_x(near_y[:half]), over_y(near_x[half:])
    mine = [column, near_x, near_y, far_low, far_high]
    return mine + [over_core(v) for v in mine]


def add(a, b):
    return (a.astype(F32) + b.astype(F32)).astype(BF)


def scatter_plane(own, sib):
    got = over_core(sib)
    send_x, send_y = add(own[0, :, 1], got[0, :, 1]), add(own[1, 1], got[1, 1])
    got_x, got_y = over_x(send_x), over_y(send_y)
    low = [add(add(own[0, y, 0], got[0, y, 0]), got_x[y]) for y in range(2)]
    high = [add(add(own[1, 0, x], got[1, 0, x]), got_y[x]) for x in range(2)]
    return jnp.concatenate([add(low[0], over_y(low[1])), add(high[0], over_x(high[1]))], axis=0)


def scatter_z(column, count):
    rows = column.shape[0] // count
    return [column[:rows]] + [over_z(column[k * rows : (k + 1) * rows], k) for k in range(1, count)]


def to_rows(own, sib, dtype, row_at):
    across, far = over_y(own.astype(BF)), None
    far = over_core(across)
    return call(
        rows_kernel,
        [struct((4,) + own.shape, dtype)],
        [own, sib, across, far],
        prefetch=(row_at,),
        grid=(4,),
        maps={("out", 0): pl.BlockSpec((1,) + own.shape, lambda i, s: (s[2] ^ i, 0, 0))},
        moved=8 * own.size,
    )[0]


def on_device(
    blocks,
    block_segment,
    upstream,
    attend_master,
    attend_first,
    attend_second,
    mixing_master,
    mixing_first,
    mixing_second,
    expand_master,
    expand_first,
    expand_second,
    shrink_master,
    shrink_first,
    shrink_second,
    gains_master,
    gains_first,
    gains_second,
):
    dp_size = lax.axis_size("dp")
    count = dp_size // 2
    rows = attend_master.shape[1]
    length, width = blocks.shape[1:]
    cols = expand_master.shape[1]
    dp_at, mp_at = lax.axis_index("dp"), lax.axis_index("mp")
    where = jnp.stack([dp_at // 2, dp_at % 2, mp_at]).astype(jnp.int32)
    row_spec = pl.BlockSpec((1, length, width), lambda i, s: (s[2], 0, 0))
    gain_cols = gains_master.T

    first, second = call(
        prepare_kernel,
        [struct((rows, 512), BF), struct((rows, 2 * cols), BF)],
        [gain_cols, attend_master, mixing_master.T, expand_master, shrink_master.T],
        moved=2 << 20,
    )
    column_one = gather_z(first, count)
    second, column_one = lax.optimization_barrier((second, column_one))
    column_two = gather_z(second, count)
    pieces_one = gather_plane(column_one)
    pieces_two = gather_plane(column_two)

    segment = lax.dynamic_slice_in_dim(block_segment, mp_at, 1, 0)
    tiles = length // TILE
    h, qkvo, probs, weights = call(
        functools.partial(attention_kernel, count, rows),
        [
            struct((length, width), F32),
            struct((length, 2048), BF),
            struct((8, tiles, TILE, 3 * TILE), BF),
            struct((width, 2048), BF),
        ],
        [blocks, segment.reshape(length, 1), segment, *pieces_one],
        prefetch=(where,),
        maps={0: row_spec},
        flops=6 * 10**9,
        moved=12 << 20,
        trans=10**6,
    )
    res, dh, gain_two, own_two, sib_two = call(
        functools.partial(feed_kernel, count, rows),
        [
            struct((length, width), BF),
            struct((length, width), F32),
            struct((8, width), F32),
            struct((2, 2, 2, 128, 2 * cols), BF),
            struct((2, 2, 2, 128, 2 * cols), BF),
        ],
        [h, upstream, *pieces_two],
        scratch=[
            pltpu.VMEM((4, width, cols), BF),
            pltpu.VMEM((4, width, cols), BF),
            *[pltpu.VMEM((width, length), BF)] * 4,
            pltpu.VMEM((length, width), F32),
            pltpu.VMEM((length, width), F32),
        ],
        prefetch=(where,),
        maps={1: row_spec},
        flops=8 * 10**9,
        moved=12 << 20,
        trans=10**6,
    )
    result = to_rows(res, over_core(res), BF, where)
    bg, bg_low, gain_one, own_one, sib_one = call(
        functools.partial(attention_back_kernel, count, rows),
        [
            struct((length, width), F32),
            struct((length, width), BF),
            struct((8, width), F32),
            struct((2, 2, 2, 128, 512), BF),
            struct((2, 2, 2, 128, 512), BF),
        ],
        [dh, blocks, qkvo, probs, weights],
        scratch=[
            pltpu.VMEM((width, length), BF),
            pltpu.VMEM((width, length), BF),
            pltpu.VMEM((length, 512), BF),
            pltpu.VMEM((length, 1536), BF),
            pltpu.VMEM((length, 128), F32),
            pltpu.VMEM((length, 128), F32),
        ],
        prefetch=(where,),
        maps={1: row_spec},
        flops=8 * 10**9,
        moved=12 << 20,
    )
    blocks_grad = to_rows(bg, over_core(bg_low), F32, where)

    terms_two = scatter_z(scatter_plane(own_two, sib_two), count)
    terms_one = scatter_z(scatter_plane(own_one, sib_one), count)
    gain_sum = jnp.concatenate([gain_one[:1], gain_two[:1]], axis=0)
    for bit in (1, 2):
        gain_sum = gain_sum + lax.ppermute(gain_sum, "mp", [(i, i ^ bit) for i in range(4)])
    bit = 1
    while bit < dp_size:
        gain_sum = gain_sum + lax.ppermute(gain_sum, "dp", [(i, i ^ bit) for i in range(dp_size)])
        bit *= 2

    def quad(shape):
        return [struct(shape, F32)] * 3 + [struct(shape, BF)]

    feed_new = call(
        functools.partial(feed_update_kernel, count),
        quad((rows, cols)) * 2,
        [
            *terms_two,
            gain_cols,
            expand_master,
            expand_first,
            expand_second,
            shrink_master.T,
            shrink_first.T,
            shrink_second.T,
        ],
        moved=3 << 20,
    )
    attention_new = call(
        functools.partial(attention_update_kernel, count),
        quad(attend_master.shape) + quad((rows, 128)),
        [
            *terms_one,
            gain_cols,
            attend_master,
            attend_first,
            attend_second,
            mixing_master.T,
            mixing_first.T,
            mixing_second.T,
        ],
        moved=3 << 20,
    )
    gain_grad = lax.dynamic_slice_in_dim(gain_sum, dp_at * rows, rows, 1) / gains_master.astype(BF).astype(F32)
    gains_new = adam(gains_master, gains_first, gains_second, gain_grad, 0.25, 0.0)
    return (
        result,
        blocks_grad,
        *attention_new[:4],
        *[a.T for a in attention_new[4:]],
        *feed_new[:4],
        *[a.T for a in feed_new[4:]],
        *gains_new,
        gains_new[0].astype(BF),
    )


def solution(mesh):
    rows = P("dp", None, None)
    attend, mixing, expand, gains = P(None, "dp", "mp"), P("mp", "dp"), P("dp", "mp"), P(None, "dp")
    kinds = (attend, mixing, expand, mixing, gains)
    in_specs = (rows, P("dp", None), rows) + tuple(k for k in kinds for _ in range(3))
    out_specs = (rows, rows) + tuple(k for k in kinds for _ in range(4))
    return jax.shard_map(on_device, mesh=mesh, in_specs=in_specs, out_specs=out_specs, check_vma=False)
```

```python
import functools

import jax
import jax.numpy as jnp
from jax import lax
from jax.experimental import pallas as pl
from jax.experimental.pallas import tpu as pltpu
from jax.sharding import PartitionSpec as P

HD = 64
STEP = 5
TILE = 128
EPS = 1e-06
GELU = 0.79788456
CUBIC = 0.044715
BF = jnp.bfloat16
F32 = jnp.float32


def nn(a, b):
    return lax.dot_general(a, b, (((1,), (0,)), ((), ())), preferred_element_type=F32)


def nt(a, b):
    return lax.dot_general(a, b, (((1,), (1,)), ((), ())), preferred_element_type=F32)


def tn(a, b):
    return lax.dot_general(a, b, (((0,), (0,)), ((), ())), preferred_element_type=F32)


def root_scale(values):
    return lax.rsqrt(jnp.mean(values * values, axis=-1, keepdims=True) + EPS)


def call(body, outs, ins, where, scratch=(), outside=(), limit=24, flops=0, moved=0, trans=0):
    vmem = pl.BlockSpec(memory_space=pltpu.VMEM)
    specs = [pl.BlockSpec(memory_space=pltpu.HBM) if k in outside else vmem for k in range(len(ins))]
    return pl.pallas_call(
        body,
        out_shape=outs,
        in_specs=[pl.BlockSpec(memory_space=pltpu.SMEM)] + specs,
        out_specs=[vmem] * len(outs),
        scratch_shapes=list(scratch),
        compiler_params=pltpu.CompilerParams(vmem_limit_bytes=limit * 1024 * 1024),
        cost_estimate=pl.CostEstimate(flops=flops, bytes_accessed=moved, transcendentals=trans),
    )(where, *ins)


def row_copy(array, row, target, sem):
    return pltpu.make_async_copy(array.at[row], target, sem)


def order_of_blocks(count):
    steps = range(1, count // 2)
    first = [(0, 0), (1, 0), (0, count // 2)] + [(c, k) for k in steps for c in (0, 1)]
    return first + [(1, count // 2)] + [(1 - c, -k) for k in steps for c in (0, 1)]


def place(pieces, core, z, x, count, rows, store):
    own, near, near_too, far, far_too = pieces
    half = far.shape[1]
    for ref, flip, x_off, y_off, at_column in (
        (own, 0, 0, 0, 0),
        (near, 0, 1 - core, core, 0),
        (near_too, 1, core, 1 - core, 0),
        (far, 0, 1, 1, core * half),
        (far_too, 1, 1, 1, (1 - core) * half),
    ):
        step = (2 * core - 1) * (1 - 2 * flip)
        x_at = lax.rem(x + x_off, 2)
        for number, (distance, k) in enumerate(order_of_blocks(count)):
            z_at = lax.rem(z + count + step * k, count)
            at = pl.multiple_of((z_at * 2 + x_at) * rows, rows)
            group = (distance ^ flip) + 2 * y_off
            for c in range(0, ref.shape[1], 128):
                store(group, at, at_column + c, ref[number * rows : (number + 1) * rows, c : c + 128])


def in_relative_rows(source, target, z, x, count, rows, x_off):
    x_at = lax.rem(x + x_off, 2)
    for k in range(count):
        z_at = lax.rem(z + k, count)
        at = pl.multiple_of((z_at * 2 + x_at) * rows, rows)
        target[k * rows : (k + 1) * rows, :] = source[pl.ds(at, rows), :]


def attention_kernel(count, rows, place_ref, x_any, seg_ref, *refs):
    h_ref, q_ref, k_ref, v_ref, o_ref, p_ref, w_ref, x_row, flat, o_flat, sem = refs[5:]
    z, x = place_ref[0], place_ref[1]
    copy = row_copy(x_any, place_ref[2], x_row, sem)
    copy.start()

    def store(group, at, c, block):
        w_ref[pl.ds(at, rows), pl.ds(pl.multiple_of(c * 4 + group * 128, 128), 128)] = block

    place(refs[:5], lax.rem(place_ref[2], 2), z, x, count, rows, store)
    copy.wait()
    states = x_row[...].astype(F32)
    unit = (states * root_scale(states)).astype(BF)
    v = nn(unit, w_ref[:, 1024:1536]).astype(BF)
    v_ref[...] = v
    flat[...] = v.T
    q_ref[...] = (nn(unit, w_ref[:, :512]) * HD**-0.5).astype(BF)
    k_ref[...] = nn(unit, w_ref[:, 512:1024]).astype(BF)
    lane = lax.broadcasted_iota(jnp.int32, (1, 128), 1)
    sides = [(lane // HD == j).astype(BF) for j in range(2)]
    tiles = q_ref.shape[0] // TILE
    segment = seg_ref[pl.ds(place_ref[2], 1), :]
    down = [column(segment[:, i * TILE : (i + 1) * TILE]) for i in range(tiles)]
    for i in range(tiles):
        first, last = max(0, i - 1), min(tiles, i + 2)
        window = slice(first * TILE, last * TILE)
        here = slice(i * TILE, (i + 1) * TILE)
        mask = jnp.concatenate(down[first:last], axis=0) == segment[:, here]
        for m in range(4):
            at = slice(m * 128, m * 128 + 128)
            q, k = q_ref[here, at], k_ref[window, at]
            for j in range(2):
                s = jnp.where(mask, nt(k, q * sides[j]), -1e30)
                e = jnp.exp(s - jnp.max(s, axis=0, keepdims=True))
                p = (e * (1.0 / jnp.sum(e, axis=0, keepdims=True))).astype(BF)
                p_ref[m * 2 + j, i, : s.shape[0], :] = p
                head = slice(m * 128 + j * HD, m * 128 + (j + 1) * HD)
                o_flat[head, here] = nn(flat[head, window], p).astype(BF)
    o = o_flat[...].T
    o_ref[...] = o
    h_ref[...] = states + nt(o, w_ref[:, 1536:2048])


def feed_kernel(count, rows, place_ref, h_ref, c_any, *refs):
    far_own, far_sib, g_ref, dz_ref, w_ref, u_near, c_near = refs[5:12]
    c_row, u_flat, c_flat, u_far, c_far, sem = refs[12:]
    z, x = place_ref[0], place_ref[1]
    width = w_ref.shape[1] // 2
    cols = width // 4
    copy = row_copy(c_any, place_ref[2], c_row, sem)
    copy.start()

    def store(group, at, c, block):
        to = c // cols * width + group * cols + c % cols if isinstance(c, int) else None
        if to is None:
            to = lax.div(c, cols) * width + group * cols + lax.rem(c, cols)
        w_ref[pl.ds(at, rows), pl.ds(pl.multiple_of(to, 128), 128)] = block

    place(refs[:5], lax.rem(place_ref[2], 2), z, x, count, rows, store)
    h = h_ref[...]
    low = (h * root_scale(h)).astype(BF)
    u_flat[...] = low.T
    copy.wait()
    back = c_row[...]
    c_flat[...] = back.T
    for source, near, far in ((u_flat, u_near, u_far), (c_flat, c_near, c_far)):
        in_relative_rows(source, near, z, x, count, rows, 0)
        in_relative_rows(source, far, z, x, count, rows, 1)
    for m in range(4):
        at = slice(m * cols, (m + 1) * cols)
        inner = nn(low, w_ref[:, at])
        square = inner * inner
        bent = jnp.tanh(inner * (GELU + GELU * CUBIC * square))
        half = 0.5 + 0.5 * bent
        g_ref[:, at] = (inner * half).astype(BF)
        slope = half + (inner * half) * (1.0 - bent) * (GELU + 3.0 * GELU * CUBIC * square)
        dz_ref[:, at] = (nn(back, w_ref[:, width + m * cols : width + (m + 1) * cols]) * slope).astype(BF)
        target = (far_own, far_sib)[m % 2]
        target[0, m // 2] = nn(u_far[...], dz_ref[:, at]).astype(BF)
        target[1, m // 2] = nn(c_far[...], g_ref[:, at]).astype(BF)


def feed_rest_kernel(place_ref, h_ref, g_ref, dz_ref, w_ref, u_near, c_near, c_any, *refs):
    near_own, near_sib, row_ref, dh_ref, gain_ref, c_row, sem = refs
    width = w_ref.shape[1] // 2
    cols = width // 4
    copy = row_copy(c_any, place_ref[2], c_row, sem)
    copy.start()
    h = h_ref[...]
    row_ref[...] = (h + nt(g_ref[...], w_ref[:, width:])).astype(BF)
    pushed = nt(dz_ref[...], w_ref[:, :width])
    for m in range(4):
        at = slice(m * cols, (m + 1) * cols)
        target = (near_own, near_sib)[m % 2]
        target[0, m // 2] = nn(u_near[...], dz_ref[:, at]).astype(BF)
        target[1, m // 2] = nn(c_near[...], g_ref[:, at]).astype(BF)
    scale = root_scale(h)
    unit = h * scale
    both = pushed * unit
    gain_ref[...] = jnp.broadcast_to(jnp.sum(both, axis=0, keepdims=True), gain_ref.shape)
    copy.wait()
    back = c_row[...].astype(F32)
    dh_ref[...] = back + scale * (pushed - unit * jnp.mean(both, axis=-1, keepdims=True))


def attention_back_kernel(count, rows, place_ref, x_any, dh_ref, q_ref, k_ref, v_ref, o_ref, p_ref, w_ref, *refs):
    gain_in, bg_ref, row_ref, near_own, far_own, near_sib, far_sib = refs[:7]
    x_row, flat_d, flat_u, near, far, do_ref, k_flat, dq_flat, ds_ref, dqkv, sem = refs[7:]
    z, x = place_ref[0], place_ref[1]
    copy = row_copy(x_any, place_ref[2], x_row, sem)
    copy.start()
    low = dh_ref[...].astype(BF)
    do_ref[...] = nn(low, w_ref[:, 1536:2048]).astype(BF)
    k_flat[...] = k_ref[...].T
    flat_d[...] = low.T

    def products(part, right):
        at = slice(part * 128, part * 128 + 128)
        for left, targets in ((near, (near_own, near_sib)), (far, (far_own, far_sib))):
            value = nn(left[...], right)
            for m in range(4):
                targets[m % 2][m // 2, : left.shape[0], at] = value[:, m * 128 : m * 128 + 128].astype(BF)

    in_relative_rows(flat_d, near, z, x, count, rows, 0)
    in_relative_rows(flat_d, far, z, x, count, rows, 1)
    products(3, o_ref[...])
    copy.wait()
    states = x_row[...].astype(F32)
    scale = root_scale(states)
    unit = states * scale
    flat_u[...] = unit.astype(BF).T
    in_relative_rows(flat_u, near, z, x, count, rows, 0)
    in_relative_rows(flat_u, far, z, x, count, rows, 1)
    lane = lax.broadcasted_iota(jnp.int32, (1, 128), 1)
    sides = [(lane // HD == j).astype(BF) for j in range(2)]
    select = (lax.broadcasted_iota(jnp.int32, (8, 128), 1) // HD == lax.broadcasted_iota(jnp.int32, (8, 128), 0)).astype(BF)
    tiles = do_ref.shape[0] // TILE
    for m in range(4):
        at = slice(m * 128, m * 128 + 128)
        for i in range(tiles):
            first, last = max(0, i - 1), min(tiles, i + 2)
            window = slice(first * TILE, last * TILE)
            here = slice(i * TILE, (i + 1) * TILE)
            v, do = v_ref[window, at], do_ref[here, at]
            delta = nt(select, do * o_ref[here, at])
            for j in range(2):
                p = p_ref[m * 2 + j, i, : v.shape[0], :].astype(F32)
                ds = (p * (nt(v, do * sides[j]) - delta[j : j + 1, :])).astype(BF)
                ds_ref[j, i, : v.shape[0], :] = ds
                head = slice(m * 128 + j * HD, m * 128 + (j + 1) * HD)
                dq_flat[head, here] = (nn(k_flat[head, window], ds) * HD**-0.5).astype(BF)
        for t in range(tiles):
            blocks = [(i, j) for i in range(max(0, t - 1), min(tiles, t + 2)) for j in range(2)]
            there = slice(t * TILE, (t + 1) * TILE)

            def rows_of(i):
                return slice((t - max(0, i - 1)) * TILE, (t - max(0, i - 1) + 1) * TILE)

            left = jnp.concatenate([ds_ref[j, i, rows_of(i), :] for i, j in blocks], axis=1)
            right = jnp.concatenate([q_ref[i * TILE : (i + 1) * TILE, at] * sides[j] for i, j in blocks], axis=0)
            dqkv[there, 512 + m * 128 : 640 + m * 128] = nn(left, right).astype(BF)
            left = jnp.concatenate([p_ref[m * 2 + j, i, rows_of(i), :] for i, j in blocks], axis=1)
            right = jnp.concatenate([do_ref[i * TILE : (i + 1) * TILE, at] * sides[j] for i, j in blocks], axis=0)
            dqkv[there, 1024 + m * 128 : 1152 + m * 128] = nn(left, right).astype(BF)
    dqkv[:, :512] = dq_flat[...].T
    for part in range(3):
        products(part, dqkv[:, part * 512 : part * 512 + 512])
    pushed = nt(dqkv[...], w_ref[:, :1536])
    both = pushed * unit
    out = dh_ref[...] + scale * (pushed - unit * jnp.mean(both, axis=-1, keepdims=True))
    bg_ref[...] = out
    row_ref[...] = out.astype(BF)
    gains = jnp.concatenate(
        [jnp.sum(both, axis=0, keepdims=True), gain_in[0:1, :], jnp.zeros((14, out.shape[1]), F32)], axis=0
    )
    width, group = out.shape[1], 2 * rows
    gains = pltpu.roll(gains, lax.rem(width - z * group, width), 1)
    lane = lax.broadcasted_iota(jnp.int32, gains.shape, 1)
    swapped = jnp.where(lax.rem(lane, group) < rows, pltpu.roll(gains, width - rows, 1), pltpu.roll(gains, rows, 1))
    here, there = jnp.where(x == 0, gains, swapped), jnp.where(x == 0, swapped, gains)
    for targets, value in (((near_own, near_sib), here), ((far_own, far_sib), there)):
        for target in targets:
            for y in range(2):
                target[y, near.shape[0] :, :] = value.astype(BF)


def column(row):
    n = row.shape[1]
    here = lax.broadcasted_iota(jnp.int32, (n, n), 0) == lax.broadcasted_iota(jnp.int32, (n, n), 1)
    return jnp.sum(jnp.where(here, row, jnp.zeros_like(row)), axis=1, keepdims=True)


def gain_column(gain, k):
    return column(gain[k : k + 1, :].astype(BF).astype(F32))


def adam(master, moment, second, gradient, rate, decay):
    moment_new = 0.5 * moment + 0.5 * gradient
    second_new = 0.6 * second + 0.4 * gradient * gradient
    update = moment_new / (1.0 - 0.5**STEP) / (jnp.sqrt(second_new / (1.0 - 0.6**STEP)) + 1e-08)
    return master - rate * (update + decay * master), moment_new, second_new


def adam_into(outs, state, gradient, rate, decay):
    master, moment, second = adam(*state, gradient, rate, decay)
    outs[0][...] = master
    outs[1][...] = moment
    outs[2][...] = second
    outs[3][...] = master.astype(BF)


def total(refs):
    whole = refs[0][...].astype(F32)
    for ref in refs[1:]:
        whole = whole + ref[...].astype(F32)
    return whole


def feed_update_kernel(count, place_ref, *refs):
    count += 1
    terms, gain, state, outs = refs[:count], refs[count], refs[count + 1 : count + 7], refs[count + 7 :]
    grad = total(terms)
    scaled = grad[0] * gain_column(gain, 1)
    adam_into(outs[:4], [r[...] for r in state[:3]], scaled, 0.05, 0.1)
    adam_into(outs[4:], [r[...] for r in state[3:]], grad[1], 0.025, 0.1)


def attention_update_kernel(count, place_ref, *refs):
    terms, state, outs = refs[:count], refs[count : count + 9], refs[count + 9 :]
    whole = total(terms)
    gain, size = state[0], state[0].shape[1]
    grad = whole[:size]
    gains = []
    for k in range(2):
        at = size + k
        parts = [ref[at : at + 1, 2 * size * n : 2 * size * n + size].astype(F32) for n, ref in enumerate(terms)]
        gains.append(sum(parts[1:], parts[0]))
    gains = jnp.concatenate(gains, axis=0) / gain[...].astype(BF).astype(F32)
    adam_into(outs[8:], [r[...] for r in state[:3]], gains, 0.25, 0.0)
    scale = gain_column(gain, 0)
    state = state[3:]
    for part in range(3):
        master, moment, second = adam(
            *[r[part] for r in state[:3]], grad[:, part * 128 : part * 128 + 128] * scale, 0.05, 0.1
        )
        outs[0][part] = master
        outs[1][part] = moment
        outs[2][part] = second
        outs[3][part] = master.astype(BF)
    adam_into(outs[4:8], [r[...] for r in state[3:]], grad[:, 384:512], 0.3, 0.1)


def prepare_kernel(place_ref, *refs):
    whole, first, second = refs[5:8]
    local, sems = refs[8:13], refs[13]
    copies = [pltpu.make_async_copy(refs[k], local[k], sems.at[k]) for k in range(5)]
    for copy in copies:
        copy.start()
    for copy in copies:
        copy.wait()
    gain, attend, mixing, expand, shrink = local
    gain_one = gain_column(gain, 0)
    gain_two = gain_column(gain, 1)
    cols = expand.shape[1]
    for part in range(3):
        first[:, part * 128 : part * 128 + 128] = (attend[part].astype(BF).astype(F32) * gain_one).astype(BF)
    first[:, 384:512] = mixing[...].astype(BF)
    second[:, :cols] = (expand[...].astype(BF).astype(F32) * gain_two).astype(BF)
    second[:, cols:] = shrink[...].astype(BF)
    whole[:, :512] = first[...]
    whole[:, 512:] = second[...]


def put_kernel(messages, place_ref, *refs):
    step = pl.program_id(0)
    for k, ref in enumerate(refs[-1 - messages : -1]):

        @pl.when(step == k)
        def _(ref=ref):
            refs[-1][0] = ref[...].astype(refs[-1].dtype)


def struct(shape, dtype):
    return jax.ShapeDtypeStruct(shape, dtype)


def over_x(value):
    n = lax.axis_size("dp")
    return lax.ppermute(value, "dp", [(i, i ^ 1) for i in range(n)])


def over_z(value, k):
    n = lax.axis_size("dp")
    return lax.ppermute(value, "dp", [(i, (i + 2 * k) % n) for i in range(n)])


def over_y(value):
    return lax.ppermute(value, "mp", [(i, i ^ 2) for i in range(4)])


def over_core(value):
    return lax.ppermute(value, "mp", [(i, i ^ 1) for i in range(4)])


def two_ways(value, first, second):
    n = lax.axis_size("dp")
    pairs = [(dp * 4 + mp, (first, second)[mp % 2](dp, mp)) for dp in range(n) for mp in range(4)]
    return lax.ppermute(value, ("dp", "mp"), [(source, dp * 4 + mp) for source, (dp, mp) in pairs])


def gather_column(block, sibling, count):
    n = 2 * count
    chip = jnp.concatenate([block, sibling], axis=0)
    got = [over_z(block, count // 2)]
    for k in range(1, count // 2):
        got.append(two_ways(chip, lambda d, m, k=k: ((d + 2 * k) % n, m), lambda d, m, k=k: ((d - 2 * k) % n, m)))
    got = jnp.concatenate(got, axis=0)
    return jnp.concatenate([chip, got, over_core(got)], axis=0)


def gather_near(column):
    return two_ways(column, lambda d, m: (d ^ 1, m), lambda d, m: (d, m ^ 2))


def gather_far(near, core):
    half = near.shape[1] // 2
    part = lax.dynamic_slice_in_dim(near, core * half, half, 1)
    return two_ways(part, lambda d, m: (d, m ^ 2), lambda d, m: (d ^ 1, m))


def after(values, *others):
    return lax.optimization_barrier((values, others))[0]


def add(*terms):
    whole = terms[0].astype(F32)
    for term in terms[1:]:
        whole = whole + term.astype(F32)
    return whole.astype(BF)


def scatter_start(grads):
    return add(grads[1], over_core(grads[3]))


def scatter_next(grads, far):
    near, got = grads[0], over_core(grads[2])
    return add(near[0], got[0], far[0]), add(near[1], got[1], far[1])


def put(array, messages, offset, where):
    size = (messages[0].shape[0] // TILE * TILE, messages[0].shape[1])
    kept = [] if offset == 0 else [array]
    return pl.pallas_call(
        functools.partial(put_kernel, len(messages)),
        out_shape=struct((4,) + size, array if offset == 0 else array.dtype),
        grid_spec=pltpu.PrefetchScalarGridSpec(
            num_scalar_prefetch=1,
            grid=(len(messages),),
            in_specs=[pl.BlockSpec(memory_space=pl.ANY)] * len(kept)
            + [pl.BlockSpec(size, lambda i, s: (0, 0))] * len(messages),
            out_specs=pl.BlockSpec((1,) + size, lambda i, s: (s[2] ^ (offset + i), 0, 0)),
        ),
        input_output_aliases={1: 0} if kept else {},
        compiler_params=pltpu.CompilerParams(vmem_limit_bytes=16 * 1024 * 1024),
        cost_estimate=pl.CostEstimate(flops=0, bytes_accessed=16 * messages[0].size, transcendentals=0),
    )(where, *kept, *messages)


def on_device(
    blocks,
    block_segment,
    upstream,
    attend_master,
    attend_first,
    attend_second,
    mixing_master,
    mixing_first,
    mixing_second,
    expand_master,
    expand_first,
    expand_second,
    shrink_master,
    shrink_first,
    shrink_second,
    gains_master,
    gains_first,
    gains_second,
):
    dp_size = lax.axis_size("dp")
    count = dp_size // 2
    rows = attend_master.shape[1]
    length, width = blocks.shape[1:]
    cols = expand_master.shape[1]
    dp_at, mp_at = lax.axis_index("dp"), lax.axis_index("mp")
    where = jnp.stack([dp_at // 2, dp_at % 2, mp_at]).astype(jnp.int32)

    masters = [gains_master, attend_master, mixing_master.T, expand_master, shrink_master.T]
    whole, first, second = call(
        prepare_kernel,
        [struct((rows, 512 + 2 * cols), BF), struct((rows, 512), BF), struct((rows, 2 * cols), BF)],
        masters,
        where,
        scratch=[pltpu.VMEM(a.shape, F32) for a in masters] + [pltpu.SemaphoreType.DMA((5,))],
        outside=range(5),
        limit=60,
        moved=2 << 20,
    )
    core = mp_at % 2
    sibling = over_core(whole)
    column_one = gather_column(first, sibling[:, :512], count)
    column_two = gather_column(second, sibling[:, 512:], count)
    near_one, near_two = gather_near(column_one), gather_near(column_two)
    far_one = gather_far(after(near_one, column_two), core)
    sib_far_one = over_core(far_one)
    tiles = length // TILE
    half = count * rows
    h, q, k, v, o, probs, weights = call(
        functools.partial(attention_kernel, count, rows),
        [
            struct((length, width), F32),
            *[struct((length, 512), BF)] * 4,
            struct((8, tiles, 3 * TILE, TILE), BF),
            struct((width, 2048), BF),
        ],
        [blocks, block_segment, column_one, near_one, over_core(near_one), far_one, sib_far_one],
        where,
        scratch=[pltpu.VMEM((length, width), BF), *[pltpu.VMEM((512, length), BF)] * 2, pltpu.SemaphoreType.DMA],
        outside=(0,),
        flops=6 * 10**9,
        moved=12 << 20,
        trans=10**6,
    )
    far_two = gather_far(after(near_two, h), core)
    pair = struct((2, 2, half, cols), BF)
    far_own, far_sib, g, dz, w_feed, u_near, c_near = call(
        functools.partial(feed_kernel, count, rows),
        [
            pair,
            pair,
            *[struct((length, 4 * cols), BF)] * 2,
            struct((width, 8 * cols), BF),
            *[struct((half, length), BF)] * 2,
        ],
        [h, upstream, column_two, near_two, over_core(near_two), far_two, over_core(far_two)],
        where,
        scratch=[
            pltpu.VMEM((length, width), BF),
            *[pltpu.VMEM((width, length), BF)] * 2,
            *[pltpu.VMEM((half, length), BF)] * 2,
            pltpu.SemaphoreType.DMA,
        ],
        outside=(1,),
        flops=4 * 10**9,
        moved=12 << 20,
        trans=10**6,
    )
    send = add(far_own, over_core(far_sib))
    g = after(g, send)
    near_own, near_sib, row, dh, gain_two = call(
        feed_rest_kernel,
        [
            pair,
            pair,
            struct((length, width), BF),
            struct((length, width), F32),
            struct((8, width), F32),
        ],
        [h, g, dz, w_feed, u_near, c_near, upstream],
        where,
        scratch=[pltpu.VMEM((length, width), BF), pltpu.SemaphoreType.DMA],
        outside=(6,),
        flops=4 * 10**9,
        moved=12 << 20,
    )
    far = over_x(send)
    row_sib, row_across = over_core(row), over_y(row)
    one = struct((2, half + 16, 512), BF)
    bg, row_low, *grads_one = call(
        functools.partial(attention_back_kernel, count, rows),
        [struct((length, width), F32), struct((length, width), BF), one, one, one, one],
        [blocks, dh, q, k, v, o, probs, weights, gain_two],
        where,
        scratch=[
            pltpu.VMEM((length, width), BF),
            *[pltpu.VMEM((width, length), BF)] * 2,
            *[pltpu.VMEM((half, length), BF)] * 2,
            pltpu.VMEM((length, 512), BF),
            *[pltpu.VMEM((512, length), BF)] * 2,
            pltpu.VMEM((2, tiles, 3 * TILE, TILE), BF),
            pltpu.VMEM((length, 1536), BF),
            pltpu.SemaphoreType.DMA,
        ],
        outside=(0,),
        flops=8 * 10**9,
        moved=12 << 20,
    )
    bg, row_low, grads_one = after((bg, row_low, grads_one), row_across)
    result = put(BF, [row, row_sib], 0, where)
    result = put(result, [row_across, over_core(row_across)], 2, where)
    send_one = scatter_start(grads_one)
    far_one = over_x(send_one)
    low_sib, low_across = over_core(row_low), over_y(row_low)
    low_far = over_core(after(low_across, far_one))
    bg = put(F32, [bg, low_sib], 0, where)
    blocks_grad = put(bg, [low_across, low_far], 2, where)

    got = over_core(near_sib)
    units = [
        add(*[part[:, :, k * rows : (k + 1) * rows] for part in (near_own, got, far)]) for k in range(count)
    ]
    units = [over_z(unit, k) if k else unit for k, unit in enumerate(units)]
    kept_one, send_one_y = scatter_next(grads_one, far_one)
    units = after(units, far_one, result)
    send = add(*[unit[:, 1] for unit in units])
    terms_two = [unit[:, 0] for unit in units] + [over_y(send)]
    sum_one = add(kept_one, over_y(send_one_y))
    parts = [jnp.concatenate([sum_one[k * rows : (k + 1) * rows], sum_one[half:]], axis=0) for k in range(count)]
    terms_one = [over_z(part, k) if k else part for k, part in enumerate(parts)]

    def quad(shape):
        return [struct(shape, F32)] * 3 + [struct(shape, BF)]

    feed_new = call(
        functools.partial(feed_update_kernel, count),
        quad((rows, cols)) * 2,
        [
            *terms_two,
            gains_master,
            expand_master,
            expand_first,
            expand_second,
            shrink_master.T,
            shrink_first.T,
            shrink_second.T,
        ],
        where,
        moved=3 << 20,
    )
    terms_one = after(terms_one, feed_new[0], blocks_grad)
    attention_new = call(
        functools.partial(attention_update_kernel, count),
        quad(attend_master.shape) + quad((rows, 128)) + quad((2, rows)),
        [
            *terms_one,
            gains_master,
            gains_first,
            gains_second,
            attend_master,
            attend_first,
            attend_second,
            mixing_master.T,
            mixing_first.T,
            mixing_second.T,
        ],
        where,
        moved=3 << 20,
    )
    return (
        result,
        blocks_grad,
        *attention_new[:4],
        *[a.T for a in attention_new[4:8]],
        *feed_new[:4],
        *[a.T for a in feed_new[4:]],
        *attention_new[8:],
    )


def solution(mesh):
    rows = P("dp", None, None)
    attend, mixing, expand, gains = P(None, "dp", "mp"), P("mp", "dp"), P("dp", "mp"), P(None, "dp")
    kinds = (attend, mixing, expand, mixing, gains)
    in_specs = (rows, P("dp", None), rows) + tuple(k for k in kinds for _ in range(3))
    out_specs = (rows, rows) + tuple(k for k in kinds for _ in range(4))
    return jax.shard_map(on_device, mesh=mesh, in_specs=in_specs, out_specs=out_specs, check_vma=False)
```

```python
import functools

import jax
import jax.numpy as jnp
from jax import lax
from jax.experimental import pallas as pl
from jax.experimental.pallas import tpu as pltpu
from jax.sharding import PartitionSpec as P

HD = 64
STEP = 5
TILE = 128
EPS = 1e-06
GELU = 0.79788456
CUBIC = 0.044715
BF = jnp.bfloat16
F32 = jnp.float32


def nn(a, b):
    return lax.dot_general(a, b, (((1,), (0,)), ((), ())), preferred_element_type=F32)


def nt(a, b):
    return lax.dot_general(a, b, (((1,), (1,)), ((), ())), preferred_element_type=F32)


def tn(a, b):
    return lax.dot_general(a, b, (((0,), (0,)), ((), ())), preferred_element_type=F32)


def root_scale(values):
    return lax.rsqrt(jnp.mean(values * values, axis=-1, keepdims=True) + EPS)


def call(body, outs, ins, where, scratch=(), outside=(), out_there=(), limit=24, flops=0, moved=0, trans=0):
    vmem = pl.BlockSpec(memory_space=pltpu.VMEM)
    specs = [pl.BlockSpec(memory_space=pltpu.HBM) if k in outside else vmem for k in range(len(ins))]
    return pl.pallas_call(
        body,
        out_shape=outs,
        in_specs=[pl.BlockSpec(memory_space=pltpu.SMEM)] + specs,
        out_specs=[pl.BlockSpec(memory_space=pltpu.HBM) if k in out_there else vmem for k in range(len(outs))],
        scratch_shapes=list(scratch),
        compiler_params=pltpu.CompilerParams(vmem_limit_bytes=limit * 1024 * 1024),
        cost_estimate=pl.CostEstimate(flops=flops, bytes_accessed=moved, transcendentals=trans),
    )(where, *ins)


def order_of_blocks(count):
    steps = range(1, count // 2)
    first = [(0, 0), (1, 0), (0, count // 2)] + [(c, k) for k in steps for c in (0, 1)]
    return first + [(1, count // 2)] + [(1 - c, -k) for k in steps for c in (0, 1)]


def place(pieces, core, z, x, count, rows, store):
    own, near, near_too, far, far_too = pieces
    half = far.shape[1]
    for ref, flip, x_off, y_off, at_column in (
        (own, 0, 0, 0, 0),
        (near, 0, 1 - core, core, 0),
        (near_too, 1, core, 1 - core, 0),
        (far, 0, 1, 1, core * half),
        (far_too, 1, 1, 1, (1 - core) * half),
    ):
        step = (2 * core - 1) * (1 - 2 * flip)
        x_at = lax.rem(x + x_off, 2)
        for number, (distance, k) in enumerate(order_of_blocks(count)):
            z_at = lax.rem(z + count + step * k, count)
            at = pl.multiple_of((z_at * 2 + x_at) * rows, rows)
            group = (distance ^ flip) + 2 * y_off
            for c in range(0, ref.shape[1], 128):
                store(group, at, at_column + c, ref[number * rows : (number + 1) * rows, c : c + 128])


def in_relative_rows(source, target, z, x, count, rows, x_off):
    x_at = lax.rem(x + x_off, 2)
    for k in range(count):
        z_at = lax.rem(z + k, count)
        at = pl.multiple_of((z_at * 2 + x_at) * rows, rows)
        target[k * rows : (k + 1) * rows, :] = source[pl.ds(at, rows), :]


def attention_kernel(count, rows, place_ref, x_row, seg_ref, *refs):
    h_ref, q_ref, k_ref, v_ref, o_ref, p_ref, w_ref, flat, o_flat = refs[5:]
    z, x = place_ref[0], place_ref[1]

    def store(group, at, c, block):
        w_ref[pl.ds(at, rows), pl.ds(pl.multiple_of(c * 4 + group * 128, 128), 128)] = block

    place(refs[:5], lax.rem(place_ref[2], 2), z, x, count, rows, store)
    states = x_row[...].astype(F32)
    unit = (states * root_scale(states)).astype(BF)
    v = nn(unit, w_ref[:, 1024:1536]).astype(BF)
    v_ref[...] = v
    flat[...] = v.T
    q_ref[...] = (nn(unit, w_ref[:, :512]) * HD**-0.5).astype(BF)
    k_ref[...] = nn(unit, w_ref[:, 512:1024]).astype(BF)
    lane = lax.broadcasted_iota(jnp.int32, (1, 128), 1)
    sides = [(lane // HD == j).astype(BF) for j in range(2)]
    tiles = q_ref.shape[0] // TILE
    segment = seg_ref[pl.ds(place_ref[2], 1), :]
    down = [column(segment[:, i * TILE : (i + 1) * TILE]) for i in range(tiles)]
    for i in range(tiles):
        first, last = max(0, i - 1), min(tiles, i + 2)
        window = slice(first * TILE, last * TILE)
        here = slice(i * TILE, (i + 1) * TILE)
        mask = jnp.concatenate(down[first:last], axis=0) == segment[:, here]
        for m in range(4):
            at = slice(m * 128, m * 128 + 128)
            q, k = q_ref[here, at], k_ref[window, at]
            for j in range(2):
                s = jnp.where(mask, nt(k, q * sides[j]), -1e30)
                e = jnp.exp(s - jnp.max(s, axis=0, keepdims=True))
                p = (e * (1.0 / jnp.sum(e, axis=0, keepdims=True))).astype(BF)
                p_ref[m * 2 + j, i, : s.shape[0], :] = p
                head = slice(m * 128 + j * HD, m * 128 + (j + 1) * HD)
                o_flat[head, here] = nn(flat[head, window], p).astype(BF)
    o = o_flat[...].T
    o_ref[...] = o
    h_ref[...] = states + nt(o, w_ref[:, 1536:2048])


def feed_kernel(count, rows, place_ref, h_ref, c_row, *refs):
    far_refs, (g_ref, dz_ref, w_ref, u_near, c_near, row_ref) = refs[5:9], refs[9:15]
    u_flat, c_flat, u_far, c_far = refs[15:]
    z, x = place_ref[0], place_ref[1]
    width = w_ref.shape[1] // 2
    cols = width // 4

    def store(group, at, c, block):
        to = c // cols * width + group * cols + c % cols if isinstance(c, int) else None
        if to is None:
            to = lax.div(c, cols) * width + group * cols + lax.rem(c, cols)
        w_ref[pl.ds(at, rows), pl.ds(pl.multiple_of(to, 128), 128)] = block

    place(refs[:5], lax.rem(place_ref[2], 2), z, x, count, rows, store)
    h = h_ref[...]
    low = (h * root_scale(h)).astype(BF)
    u_flat[...] = low.T
    back = c_row[...]
    c_flat[...] = back.T
    for source, near, far in ((u_flat, u_near, u_far), (c_flat, c_near, c_far)):
        in_relative_rows(source, near, z, x, count, rows, 0)
        in_relative_rows(source, far, z, x, count, rows, 1)
    for m in range(4):
        at = slice(m * cols, (m + 1) * cols)
        inner = nn(low, w_ref[:, at])
        square = inner * inner
        bent = jnp.tanh(inner * (GELU + GELU * CUBIC * square))
        half = 0.5 + 0.5 * bent
        g_ref[:, at] = (inner * half).astype(BF)
        slope = half + (inner * half) * (1.0 - bent) * (GELU + 3.0 * GELU * CUBIC * square)
        dz_ref[:, at] = (nn(back, w_ref[:, width + m * cols : width + (m + 1) * cols]) * slope).astype(BF)
        far_refs[m % 2][m // 2] = nn(u_far[...], dz_ref[:, at]).astype(BF)
        far_refs[2 + m % 2][m // 2] = nn(c_far[...], g_ref[:, at]).astype(BF)
    row_ref[...] = (h + nt(g_ref[...], w_ref[:, width:])).astype(BF)


def feed_rest_kernel(place_ref, h_ref, g_ref, dz_ref, w_ref, u_near, c_near, c_row, *refs):
    near_own, near_sib, dh_ref, gain_ref = refs
    width = w_ref.shape[1] // 2
    cols = width // 4
    h = h_ref[...]
    pushed = nt(dz_ref[...], w_ref[:, :width])
    for m in range(4):
        at = slice(m * cols, (m + 1) * cols)
        target = (near_own, near_sib)[m % 2]
        target[0, m // 2] = nn(u_near[...], dz_ref[:, at]).astype(BF)
        target[1, m // 2] = nn(c_near[...], g_ref[:, at]).astype(BF)
    scale = root_scale(h)
    unit = h * scale
    both = pushed * unit
    gain_ref[...] = jnp.broadcast_to(jnp.sum(both, axis=0, keepdims=True), gain_ref.shape)
    back = c_row[...].astype(F32)
    dh_ref[...] = back + scale * (pushed - unit * jnp.mean(both, axis=-1, keepdims=True))


def attention_back_kernel(count, rows, place_ref, x_row, dh_ref, q_ref, k_ref, v_ref, o_ref, p_ref, w_ref, *refs):
    gain_in, bg_ref, row_ref, near_own, far_own, near_sib, far_sib = refs[:7]
    flat_d, flat_u, near, far, do_ref, k_flat, dq_flat, ds_ref, dqkv = refs[7:]
    z, x = place_ref[0], place_ref[1]
    low = dh_ref[...].astype(BF)
    do_ref[...] = nn(low, w_ref[:, 1536:2048]).astype(BF)
    k_flat[...] = k_ref[...].T
    flat_d[...] = low.T

    def products(part, right):
        at = slice(part * 128, part * 128 + 128)
        for left, targets in ((near, (near_own, near_sib)), (far, (far_own, far_sib))):
            value = nn(left[...], right)
            for m in range(4):
                targets[m % 2][m // 2, : left.shape[0], at] = value[:, m * 128 : m * 128 + 128].astype(BF)

    in_relative_rows(flat_d, near, z, x, count, rows, 0)
    in_relative_rows(flat_d, far, z, x, count, rows, 1)
    products(3, o_ref[...])
    states = x_row[...].astype(F32)
    scale = root_scale(states)
    unit = states * scale
    flat_u[...] = unit.astype(BF).T
    in_relative_rows(flat_u, near, z, x, count, rows, 0)
    in_relative_rows(flat_u, far, z, x, count, rows, 1)
    lane = lax.broadcasted_iota(jnp.int32, (1, 128), 1)
    sides = [(lane // HD == j).astype(BF) for j in range(2)]
    select = (lax.broadcasted_iota(jnp.int32, (8, 128), 1) // HD == lax.broadcasted_iota(jnp.int32, (8, 128), 0)).astype(BF)
    tiles = do_ref.shape[0] // TILE
    for m in range(4):
        at = slice(m * 128, m * 128 + 128)
        for i in range(tiles):
            first, last = max(0, i - 1), min(tiles, i + 2)
            window = slice(first * TILE, last * TILE)
            here = slice(i * TILE, (i + 1) * TILE)
            v, do = v_ref[window, at], do_ref[here, at]
            delta = nt(select, do * o_ref[here, at])
            for j in range(2):
                p = p_ref[m * 2 + j, i, : v.shape[0], :].astype(F32)
                ds = (p * (nt(v, do * sides[j]) - delta[j : j + 1, :])).astype(BF)
                ds_ref[j, i, : v.shape[0], :] = ds
                head = slice(m * 128 + j * HD, m * 128 + (j + 1) * HD)
                dq_flat[head, here] = (nn(k_flat[head, window], ds) * HD**-0.5).astype(BF)
        for t in range(tiles):
            blocks = [(i, j) for i in range(max(0, t - 1), min(tiles, t + 2)) for j in range(2)]
            there = slice(t * TILE, (t + 1) * TILE)

            def rows_of(i):
                return slice((t - max(0, i - 1)) * TILE, (t - max(0, i - 1) + 1) * TILE)

            left = jnp.concatenate([ds_ref[j, i, rows_of(i), :] for i, j in blocks], axis=1)
            right = jnp.concatenate([q_ref[i * TILE : (i + 1) * TILE, at] * sides[j] for i, j in blocks], axis=0)
            dqkv[there, 512 + m * 128 : 640 + m * 128] = nn(left, right).astype(BF)
            left = jnp.concatenate([p_ref[m * 2 + j, i, rows_of(i), :] for i, j in blocks], axis=1)
            right = jnp.concatenate([do_ref[i * TILE : (i + 1) * TILE, at] * sides[j] for i, j in blocks], axis=0)
            dqkv[there, 1024 + m * 128 : 1152 + m * 128] = nn(left, right).astype(BF)
    dqkv[:, :512] = dq_flat[...].T
    for part in range(3):
        products(part, dqkv[:, part * 512 : part * 512 + 512])
    pushed = nt(dqkv[...], w_ref[:, :1536])
    both = pushed * unit
    out = dh_ref[...] + scale * (pushed - unit * jnp.mean(both, axis=-1, keepdims=True))
    bg_ref[...] = out
    row_ref[...] = out.astype(BF)
    gains = jnp.concatenate(
        [jnp.sum(both, axis=0, keepdims=True), gain_in[0:1, :], jnp.zeros((14, out.shape[1]), F32)], axis=0
    )
    width, group = out.shape[1], 2 * rows
    gains = pltpu.roll(gains, lax.rem(width - z * group, width), 1)
    lane = lax.broadcasted_iota(jnp.int32, gains.shape, 1)
    swapped = jnp.where(lax.rem(lane, group) < rows, pltpu.roll(gains, width - rows, 1), pltpu.roll(gains, rows, 1))
    here, there = jnp.where(x == 0, gains, swapped), jnp.where(x == 0, swapped, gains)
    for targets, value in (((near_own, near_sib), here), ((far_own, far_sib), there)):
        for target in targets:
            for y in range(2):
                target[y, near.shape[0] :, :] = value.astype(BF)


def column(row):
    n = row.shape[1]
    here = lax.broadcasted_iota(jnp.int32, (n, n), 0) == lax.broadcasted_iota(jnp.int32, (n, n), 1)
    return jnp.sum(jnp.where(here, row, jnp.zeros_like(row)), axis=1, keepdims=True)


def gain_column(gain, k):
    return column(gain[k : k + 1, :].astype(BF).astype(F32))


def adam(master, moment, second, gradient, rate, decay):
    moment_new = 0.5 * moment + 0.5 * gradient
    second_new = 0.6 * second + 0.4 * gradient * gradient
    update = moment_new / (1.0 - 0.5**STEP) / (jnp.sqrt(second_new / (1.0 - 0.6**STEP)) + 1e-08)
    return master - rate * (update + decay * master), moment_new, second_new


def adam_into(outs, state, gradient, rate, decay):
    master, moment, second = adam(*state, gradient, rate, decay)
    outs[0][...] = master
    outs[1][...] = moment
    outs[2][...] = second
    outs[3][...] = master.astype(BF)


def total(refs):
    whole = refs[0][...].astype(F32)
    for ref in refs[1:]:
        whole = whole + ref[...].astype(F32)
    return whole


def feed_update_kernel(count, place_ref, *refs):
    terms_e, terms_s, refs = refs[:count], refs[count : 2 * count], refs[2 * count :]
    gain, state, outs = refs[0], refs[1:7], refs[7:]
    scaled = total(terms_e) * gain_column(gain, 1)
    adam_into(outs[:4], [r[...] for r in state[:3]], scaled, 0.05, 0.1)
    adam_into(outs[4:], [r[...] for r in state[3:]], total(terms_s), 0.025, 0.1)


def attention_update_kernel(count, place_ref, *refs):
    terms, state, outs = refs[:count], refs[count : count + 9], refs[count + 9 :]
    whole = total(terms)
    gain, size = state[0], state[0].shape[1]
    grad = whole[:size]
    gains = []
    for k in range(2):
        at = size + k
        parts = [ref[at : at + 1, 2 * size * n : 2 * size * n + size].astype(F32) for n, ref in enumerate(terms)]
        gains.append(sum(parts[1:], parts[0]))
    gains = jnp.concatenate(gains, axis=0) / gain[...].astype(BF).astype(F32)
    adam_into(outs[8:], [r[...] for r in state[:3]], gains, 0.25, 0.0)
    scale = gain_column(gain, 0)
    state = state[3:]
    for part in range(3):
        master, moment, second = adam(
            *[r[part] for r in state[:3]], grad[:, part * 128 : part * 128 + 128] * scale, 0.05, 0.1
        )
        outs[0][part] = master
        outs[1][part] = moment
        outs[2][part] = second
        outs[3][part] = master.astype(BF)
    adam_into(outs[4:8], [r[...] for r in state[3:]], grad[:, 384:512], 0.3, 0.1)


def prepare_kernel(place_ref, *refs):
    whole, first, second, x_row, c_row = refs[7:12]
    local, sems = refs[12:17], refs[17]
    rows = [pltpu.make_async_copy(refs[5 + k].at[place_ref[2]], (x_row, c_row)[k], sems.at[5 + k]) for k in range(2)]
    copies = [pltpu.make_async_copy(refs[k], local[k], sems.at[k]) for k in range(5)]
    for copy in copies + rows:
        copy.start()
    for copy in copies:
        copy.wait()
    gain, attend, mixing, expand, shrink = local
    gain_one = gain_column(gain, 0)
    gain_two = gain_column(gain, 1)
    cols = expand.shape[1]
    for part in range(3):
        first[:, part * 128 : part * 128 + 128] = (attend[part].astype(BF).astype(F32) * gain_one).astype(BF)
    first[:, 384:512] = mixing[...].astype(BF)
    second[:, :cols] = (expand[...].astype(BF).astype(F32) * gain_two).astype(BF)
    second[:, cols:] = shrink[...].astype(BF)
    whole[:, :512] = first[...]
    whole[:, 512:] = second[...]
    for copy in rows:
        copy.wait()


def put_kernel(messages, place_ref, *refs):
    step = pl.program_id(0)
    for k, ref in enumerate(refs[-1 - messages : -1]):

        @pl.when(step == k)
        def _(ref=ref):
            refs[-1][0] = ref[...].astype(refs[-1].dtype)


def struct(shape, dtype):
    return jax.ShapeDtypeStruct(shape, dtype)


def over_x(value):
    n = lax.axis_size("dp")
    return lax.ppermute(value, "dp", [(i, i ^ 1) for i in range(n)])


def over_z(value, k):
    n = lax.axis_size("dp")
    return lax.ppermute(value, "dp", [(i, (i + 2 * k) % n) for i in range(n)])


def over_y(value):
    return lax.ppermute(value, "mp", [(i, i ^ 2) for i in range(4)])


def over_core(value):
    return lax.ppermute(value, "mp", [(i, i ^ 1) for i in range(4)])


def two_ways(value, first, second):
    n = lax.axis_size("dp")
    pairs = [(dp * 4 + mp, (first, second)[mp % 2](dp, mp)) for dp in range(n) for mp in range(4)]
    return lax.ppermute(value, ("dp", "mp"), [(source, dp * 4 + mp) for source, (dp, mp) in pairs])


def gather_column(block, sibling, count):
    n = 2 * count
    chip = jnp.concatenate([block, sibling], axis=0)
    got = [over_z(block, count // 2)]
    for k in range(1, count // 2):
        got.append(two_ways(chip, lambda d, m, k=k: ((d + 2 * k) % n, m), lambda d, m, k=k: ((d - 2 * k) % n, m)))
    got = jnp.concatenate(got, axis=0)
    return jnp.concatenate([chip, got, over_core(got)], axis=0)


def gather_near(column):
    return two_ways(column, lambda d, m: (d ^ 1, m), lambda d, m: (d, m ^ 2))


def gather_far(near, core):
    half = near.shape[1] // 2
    part = lax.dynamic_slice_in_dim(near, core * half, half, 1)
    return two_ways(part, lambda d, m: (d, m ^ 2), lambda d, m: (d ^ 1, m))


def after(values, *others):
    return lax.optimization_barrier((values, others))[0]


def add(*terms):
    whole = terms[0].astype(F32)
    for term in terms[1:]:
        whole = whole + term.astype(F32)
    return whole.astype(BF)


def scatter_start(grads):
    return add(grads[1], over_core(grads[3]))


def scatter_next(grads, far):
    near, got = grads[0], over_core(grads[2])
    return add(near[0], got[0], far[0]), add(near[1], got[1], far[1])


def put(array, messages, offset, where):
    size = (messages[0].shape[0] // TILE * TILE, messages[0].shape[1])
    kept = [] if offset == 0 else [array]
    return pl.pallas_call(
        functools.partial(put_kernel, len(messages)),
        out_shape=struct((4,) + size, array if offset == 0 else array.dtype),
        grid_spec=pltpu.PrefetchScalarGridSpec(
            num_scalar_prefetch=1,
            grid=(len(messages),),
            in_specs=[pl.BlockSpec(memory_space=pl.ANY)] * len(kept)
            + [pl.BlockSpec(size, lambda i, s: (0, 0))] * len(messages),
            out_specs=pl.BlockSpec((1,) + size, lambda i, s: (s[2] ^ (offset + i), 0, 0)),
        ),
        input_output_aliases={1: 0} if kept else {},
        compiler_params=pltpu.CompilerParams(vmem_limit_bytes=16 * 1024 * 1024),
        cost_estimate=pl.CostEstimate(flops=0, bytes_accessed=16 * messages[0].size, transcendentals=0),
    )(where, *kept, *messages)


def on_device(
    blocks,
    block_segment,
    upstream,
    attend_master,
    attend_first,
    attend_second,
    mixing_master,
    mixing_first,
    mixing_second,
    expand_master,
    expand_first,
    expand_second,
    shrink_master,
    shrink_first,
    shrink_second,
    gains_master,
    gains_first,
    gains_second,
):
    dp_size = lax.axis_size("dp")
    count = dp_size // 2
    rows = attend_master.shape[1]
    length, width = blocks.shape[1:]
    cols = expand_master.shape[1]
    dp_at, mp_at = lax.axis_index("dp"), lax.axis_index("mp")
    where = jnp.stack([dp_at // 2, dp_at % 2, mp_at]).astype(jnp.int32)

    masters = [gains_master, attend_master, mixing_master.T, expand_master, shrink_master.T]
    whole, first, second, x_row, c_row = call(
        prepare_kernel,
        [struct((rows, 512 + 2 * cols), BF), struct((rows, 512), BF), struct((rows, 2 * cols), BF)]
        + [struct((length, width), BF)] * 2,
        masters + [blocks, upstream],
        where,
        scratch=[pltpu.VMEM(a.shape, F32) for a in masters] + [pltpu.SemaphoreType.DMA((7,))],
        outside=range(7),

        limit=60,
        moved=2 << 20,
    )
    core = mp_at % 2
    sibling = over_core(whole)
    column_one = gather_column(first, sibling[:, :512], count)
    column_two = gather_column(second, sibling[:, 512:], count)
    near_one = gather_near(column_one)
    near_two = gather_near(after(column_two, near_one))
    far_one = gather_far(near_one, core)
    sib_far_one = over_core(far_one)
    tiles = length // TILE
    half = count * rows
    h, q, k, v, o, probs, weights = call(
        functools.partial(attention_kernel, count, rows),
        [
            struct((length, width), F32),
            *[struct((length, 512), BF)] * 4,
            struct((8, tiles, 3 * TILE, TILE), BF),
            struct((width, 2048), BF),
        ],
        [x_row, block_segment, column_one, near_one, over_core(near_one), far_one, sib_far_one],
        where,
        scratch=[pltpu.VMEM((512, length), BF)] * 2,
        flops=6 * 10**9,
        moved=12 << 20,
        trans=10**6,
    )
    far_two = gather_far(near_two, core)
    sib_far_two = over_core(after(far_two, h))
    pair = struct((2, 2, half, cols), BF)
    *far_grads, g, dz, w_feed, u_near, c_near, row = call(
        functools.partial(feed_kernel, count, rows),
        [
            *[struct((2, half, cols), BF)] * 4,
            *[struct((length, 4 * cols), BF)] * 2,
            struct((width, 8 * cols), BF),
            *[struct((half, length), BF)] * 2,
            struct((length, width), BF),
        ],
        [h, c_row, column_two, near_two, over_core(near_two), far_two, sib_far_two],
        where,
        scratch=[*[pltpu.VMEM((width, length), BF)] * 2, *[pltpu.VMEM((half, length), BF)] * 2],
        flops=4 * 10**9,
        moved=12 << 20,
        trans=10**6,
    )
    send_x = [add(far_grads[k], over_core(far_grads[k + 1])) for k in (0, 2)]
    g = after(g, send_x)
    near_own, near_sib, dh, gain_two = call(
        feed_rest_kernel,
        [
            pair,
            pair,
            struct((length, width), F32),
            struct((8, width), F32),
        ],
        [h, g, dz, w_feed, u_near, c_near, c_row],
        where,
        flops=4 * 10**9,
        moved=12 << 20,
    )
    far = [over_x(value) for value in send_x]
    row_sib, row_across = over_core(row), over_y(row)
    one = struct((2, half + 16, 512), BF)
    bg, row_low, *grads_one = call(
        functools.partial(attention_back_kernel, count, rows),
        [struct((length, width), F32), struct((length, width), BF), one, one, one, one],
        [x_row, dh, q, k, v, o, probs, weights, gain_two],
        where,
        scratch=[
            *[pltpu.VMEM((width, length), BF)] * 2,
            *[pltpu.VMEM((half, length), BF)] * 2,
            pltpu.VMEM((length, 512), BF),
            *[pltpu.VMEM((512, length), BF)] * 2,
            pltpu.VMEM((2, tiles, 3 * TILE, TILE), BF),
            pltpu.VMEM((length, 1536), BF),
        ],
        flops=8 * 10**9,
        moved=12 << 20,
    )
    bg, row_low = after((bg, row_low), row_across)
    low_sib, low_across = over_core(row_low), over_y(row_low)
    grads_one = after(grads_one, far[1])
    result = put(BF, [row, row_sib], 0, where)
    result = put(result, [row_across, over_core(row_across)], 2, where)
    send_one = scatter_start(grads_one)
    far_one = over_x(send_one)
    low_far = over_core(after(low_across, far_one))
    bg = put(F32, [bg, low_sib], 0, where)
    blocks_grad = put(bg, [low_across, low_far], 2, where)

    got = over_core(near_sib)
    kept_one, send_one_y = scatter_next(grads_one, far_one)
    sums = []
    for k in (1, 0):
        kept, send = [add(near_own[k, y], got[k, y], far[k][y]) for y in range(2)]
        if k == 0:
            send = after(send, low_across)
        sums.append(add(kept, over_y(send)))
    sums = sums[::-1]
    sums[0] = after(sums[0], result)
    terms_two = []
    for value in sums:
        terms_two += [value[:rows]] + [over_z(value[k * rows : (k + 1) * rows], k) for k in range(1, count)]
    sum_one = add(kept_one, over_y(send_one_y))
    parts = [jnp.concatenate([sum_one[k * rows : (k + 1) * rows], sum_one[half:]], axis=0) for k in range(count)]
    terms_one = [over_z(part, k) if k else part for k, part in enumerate(parts)]

    def quad(shape):
        return [struct(shape, F32)] * 3 + [struct(shape, BF)]

    feed_new = call(
        functools.partial(feed_update_kernel, count),
        quad((rows, cols)) * 2,
        [
            *terms_two,
            gains_master,
            expand_master,
            expand_first,
            expand_second,
            shrink_master.T,
            shrink_first.T,
            shrink_second.T,
        ],
        where,
        moved=3 << 20,
    )
    terms_one = after(terms_one, feed_new[0], blocks_grad)
    attention_new = call(
        functools.partial(attention_update_kernel, count),
        quad(attend_master.shape) + quad((rows, 128)) + quad((2, rows)),
        [
            *terms_one,
            gains_master,
            gains_first,
            gains_second,
            attend_master,
            attend_first,
            attend_second,
            mixing_master.T,
            mixing_first.T,
            mixing_second.T,
        ],
        where,
        moved=3 << 20,
    )
    return (
        result,
        blocks_grad,
        *attention_new[:4],
        *[a.T for a in attention_new[4:8]],
        *feed_new[:4],
        *[a.T for a in feed_new[4:]],
        *attention_new[8:],
    )


def solution(mesh):
    rows = P("dp", None, None)
    attend, mixing, expand, gains = P(None, "dp", "mp"), P("mp", "dp"), P("dp", "mp"), P(None, "dp")
    kinds = (attend, mixing, expand, mixing, gains)
    in_specs = (rows, P("dp", None), rows) + tuple(k for k in kinds for _ in range(3))
    out_specs = (rows, rows) + tuple(k for k in kinds for _ in range(4))
    return jax.shard_map(on_device, mesh=mesh, in_specs=in_specs, out_specs=out_specs, check_vma=False)
```

```python
import functools

import jax
import jax.numpy as jnp
from jax import lax
from jax.experimental import pallas as pl
from jax.experimental.pallas import tpu as pltpu
from jax.sharding import PartitionSpec as P

HD = 64
STEP = 5
TILE = 128
EPS = 1e-06
GELU = 0.79788456
CUBIC = 0.044715
BF = jnp.bfloat16
F32 = jnp.float32


def nn(a, b):
    return lax.dot_general(a, b, (((1,), (0,)), ((), ())), preferred_element_type=F32)


def nt(a, b):
    return lax.dot_general(a, b, (((1,), (1,)), ((), ())), preferred_element_type=F32)


def tn(a, b):
    return lax.dot_general(a, b, (((0,), (0,)), ((), ())), preferred_element_type=F32)


def root_scale(values):
    return lax.rsqrt(jnp.mean(values * values, axis=-1, keepdims=True) + EPS)


def call(body, outs, ins, where, scratch=(), outside=(), out_there=(), limit=24, flops=0, moved=0, trans=0):
    vmem = pl.BlockSpec(memory_space=pltpu.VMEM)
    specs = [pl.BlockSpec(memory_space=pltpu.HBM) if k in outside else vmem for k in range(len(ins))]
    return pl.pallas_call(
        body,
        out_shape=outs,
        in_specs=[pl.BlockSpec(memory_space=pltpu.SMEM)] + specs,
        out_specs=[pl.BlockSpec(memory_space=pltpu.HBM) if k in out_there else vmem for k in range(len(outs))],
        scratch_shapes=list(scratch),
        compiler_params=pltpu.CompilerParams(vmem_limit_bytes=limit * 1024 * 1024),
        cost_estimate=pl.CostEstimate(flops=flops, bytes_accessed=moved, transcendentals=trans),
    )(where, *ins)


def order_of_blocks(count):
    steps = range(1, count // 2)
    first = [(0, 0), (1, 0), (0, count // 2)] + [(c, k) for k in steps for c in (0, 1)]
    return first + [(1, count // 2)] + [(1 - c, -k) for k in steps for c in (0, 1)]


def place(pieces, core, z, x, count, rows, store):
    own, near, near_too, far, far_too = pieces
    half = far.shape[1]
    for ref, flip, x_off, y_off, at_column in (
        (own, 0, 0, 0, 0),
        (near, 0, 1 - core, core, 0),
        (near_too, 1, core, 1 - core, 0),
        (far, 0, 1, 1, core * half),
        (far_too, 1, 1, 1, (1 - core) * half),
    ):
        step = (2 * core - 1) * (1 - 2 * flip)
        x_at = lax.rem(x + x_off, 2)
        for number, (distance, k) in enumerate(order_of_blocks(count)):
            z_at = lax.rem(z + count + step * k, count)
            at = pl.multiple_of((z_at * 2 + x_at) * rows, rows)
            group = (distance ^ flip) + 2 * y_off
            for c in range(0, ref.shape[1], 128):
                store(group, at, at_column + c, ref[number * rows : (number + 1) * rows, c : c + 128])


def in_relative_rows(source, target, z, x, count, rows, x_off):
    x_at = lax.rem(x + x_off, 2)
    for k in range(count):
        z_at = lax.rem(z + k, count)
        at = pl.multiple_of((z_at * 2 + x_at) * rows, rows)
        target[k * rows : (k + 1) * rows, :] = source[pl.ds(at, rows), :]


def attention_kernel(count, rows, place_ref, x_row, seg_ref, *refs):
    h_ref, q_ref, k_ref, v_ref, o_ref, p_ref, w_ref, flat, o_flat = refs[5:]
    z, x = place_ref[0], place_ref[1]

    def store(group, at, c, block):
        w_ref[pl.ds(at, rows), pl.ds(pl.multiple_of(c * 4 + group * 128, 128), 128)] = block

    place(refs[:5], lax.rem(place_ref[2], 2), z, x, count, rows, store)
    states = x_row[...].astype(F32)
    unit = (states * root_scale(states)).astype(BF)
    v = nn(unit, w_ref[:, 1024:1536]).astype(BF)
    v_ref[...] = v
    flat[...] = v.T
    q_ref[...] = (nn(unit, w_ref[:, :512]) * HD**-0.5).astype(BF)
    k_ref[...] = nn(unit, w_ref[:, 512:1024]).astype(BF)
    lane = lax.broadcasted_iota(jnp.int32, (1, 128), 1)
    sides = [(lane // HD == j).astype(BF) for j in range(2)]
    tiles = q_ref.shape[0] // TILE
    segment = seg_ref[pl.ds(place_ref[2], 1), :]
    down = [column(segment[:, i * TILE : (i + 1) * TILE]) for i in range(tiles)]
    for i in range(tiles):
        first, last = max(0, i - 1), min(tiles, i + 2)
        window = slice(first * TILE, last * TILE)
        here = slice(i * TILE, (i + 1) * TILE)
        mask = jnp.concatenate(down[first:last], axis=0) == segment[:, here]
        for m in range(4):
            at = slice(m * 128, m * 128 + 128)
            q, k = q_ref[here, at], k_ref[window, at]
            for j in range(2):
                s = jnp.where(mask, nt(k, q * sides[j]), -1e30)
                e = jnp.exp(s - jnp.max(s, axis=0, keepdims=True))
                p = (e * (1.0 / jnp.sum(e, axis=0, keepdims=True))).astype(BF)
                p_ref[m * 2 + j, i, : s.shape[0], :] = p
                head = slice(m * 128 + j * HD, m * 128 + (j + 1) * HD)
                o_flat[head, here] = nn(flat[head, window], p).astype(BF)
    o = o_flat[...].T
    o_ref[...] = o
    h_ref[...] = states + nt(o, w_ref[:, 1536:2048])


def feed_kernel(count, rows, place_ref, h_ref, c_row, *refs):
    far_refs, (g_ref, dz_ref, w_ref, u_near, c_near, row_ref) = refs[5:9], refs[9:15]
    u_flat, c_flat, u_far, c_far = refs[15:]
    z, x = place_ref[0], place_ref[1]
    width = w_ref.shape[1] // 2
    cols = width // 4

    def store(group, at, c, block):
        to = c // cols * width + group * cols + c % cols if isinstance(c, int) else None
        if to is None:
            to = lax.div(c, cols) * width + group * cols + lax.rem(c, cols)
        w_ref[pl.ds(at, rows), pl.ds(pl.multiple_of(to, 128), 128)] = block

    place(refs[:5], lax.rem(place_ref[2], 2), z, x, count, rows, store)
    h = h_ref[...]
    low = (h * root_scale(h)).astype(BF)
    u_flat[...] = low.T
    back = c_row[...]
    c_flat[...] = back.T
    for source, near, far in ((u_flat, u_near, u_far), (c_flat, c_near, c_far)):
        in_relative_rows(source, near, z, x, count, rows, 0)
        in_relative_rows(source, far, z, x, count, rows, 1)
    for m in range(4):
        at = slice(m * cols, (m + 1) * cols)
        inner = nn(low, w_ref[:, at])
        square = inner * inner
        bent = jnp.tanh(inner * (GELU + GELU * CUBIC * square))
        half = 0.5 + 0.5 * bent
        g_ref[:, at] = (inner * half).astype(BF)
        slope = half + (inner * half) * (1.0 - bent) * (GELU + 3.0 * GELU * CUBIC * square)
        dz_ref[:, at] = (nn(back, w_ref[:, width + m * cols : width + (m + 1) * cols]) * slope).astype(BF)
        far_refs[m % 2][m // 2] = nn(u_far[...], dz_ref[:, at]).astype(BF)
        far_refs[2 + m % 2][m // 2] = nn(c_far[...], g_ref[:, at]).astype(BF)
    row_ref[...] = (h + nt(g_ref[...], w_ref[:, width:])).astype(BF)


def feed_rest_kernel(place_ref, h_ref, g_ref, dz_ref, w_ref, u_near, c_near, c_row, *refs):
    near_own, near_sib, dh_ref, gain_ref = refs
    width = w_ref.shape[1] // 2
    cols = width // 4
    h = h_ref[...]
    pushed = nt(dz_ref[...], w_ref[:, :width])
    for m in range(4):
        at = slice(m * cols, (m + 1) * cols)
        target = (near_own, near_sib)[m % 2]
        target[0, m // 2] = nn(u_near[...], dz_ref[:, at]).astype(BF)
        target[1, m // 2] = nn(c_near[...], g_ref[:, at]).astype(BF)
    scale = root_scale(h)
    unit = h * scale
    both = pushed * unit
    gain_ref[...] = jnp.broadcast_to(jnp.sum(both, axis=0, keepdims=True), gain_ref.shape)
    back = c_row[...].astype(F32)
    dh_ref[...] = back + scale * (pushed - unit * jnp.mean(both, axis=-1, keepdims=True))


def attention_back_kernel(count, rows, place_ref, x_row, dh_ref, q_ref, k_ref, v_ref, o_ref, p_ref, w_ref, *refs):
    gain_in, bg_ref, row_ref, near_own, far_own, near_sib, far_sib = refs[:7]
    flat_d, flat_u, near, far, do_ref, k_flat, dq_flat, ds_ref, dqkv = refs[7:]
    z, x = place_ref[0], place_ref[1]
    low = dh_ref[...].astype(BF)
    do_ref[...] = nn(low, w_ref[:, 1536:2048]).astype(BF)
    k_flat[...] = k_ref[...].T
    flat_d[...] = low.T

    def products(part, right):
        at = slice(part * 128, part * 128 + 128)
        for left, targets in ((near, (near_own, near_sib)), (far, (far_own, far_sib))):
            value = nn(left[...], right)
            for m in range(4):
                targets[m % 2][m // 2, : left.shape[0], at] = value[:, m * 128 : m * 128 + 128].astype(BF)

    in_relative_rows(flat_d, near, z, x, count, rows, 0)
    in_relative_rows(flat_d, far, z, x, count, rows, 1)
    products(3, o_ref[...])
    states = x_row[...].astype(F32)
    scale = root_scale(states)
    unit = states * scale
    flat_u[...] = unit.astype(BF).T
    in_relative_rows(flat_u, near, z, x, count, rows, 0)
    in_relative_rows(flat_u, far, z, x, count, rows, 1)
    lane = lax.broadcasted_iota(jnp.int32, (1, 128), 1)
    sides = [(lane // HD == j).astype(BF) for j in range(2)]
    select = (lax.broadcasted_iota(jnp.int32, (8, 128), 1) // HD == lax.broadcasted_iota(jnp.int32, (8, 128), 0)).astype(BF)
    tiles = do_ref.shape[0] // TILE
    for m in range(4):
        at = slice(m * 128, m * 128 + 128)
        for i in range(tiles):
            first, last = max(0, i - 1), min(tiles, i + 2)
            window = slice(first * TILE, last * TILE)
            here = slice(i * TILE, (i + 1) * TILE)
            v, do = v_ref[window, at], do_ref[here, at]
            delta = nt(select, do * o_ref[here, at])
            for j in range(2):
                p = p_ref[m * 2 + j, i, : v.shape[0], :].astype(F32)
                ds = (p * (nt(v, do * sides[j]) - delta[j : j + 1, :])).astype(BF)
                ds_ref[j, i, : v.shape[0], :] = ds
                head = slice(m * 128 + j * HD, m * 128 + (j + 1) * HD)
                dq_flat[head, here] = (nn(k_flat[head, window], ds) * HD**-0.5).astype(BF)
        for t in range(tiles):
            blocks = [(i, j) for i in range(max(0, t - 1), min(tiles, t + 2)) for j in range(2)]
            there = slice(t * TILE, (t + 1) * TILE)

            def rows_of(i):
                return slice((t - max(0, i - 1)) * TILE, (t - max(0, i - 1) + 1) * TILE)

            left = jnp.concatenate([ds_ref[j, i, rows_of(i), :] for i, j in blocks], axis=1)
            right = jnp.concatenate([q_ref[i * TILE : (i + 1) * TILE, at] * sides[j] for i, j in blocks], axis=0)
            dqkv[there, 512 + m * 128 : 640 + m * 128] = nn(left, right).astype(BF)
            left = jnp.concatenate([p_ref[m * 2 + j, i, rows_of(i), :] for i, j in blocks], axis=1)
            right = jnp.concatenate([do_ref[i * TILE : (i + 1) * TILE, at] * sides[j] for i, j in blocks], axis=0)
            dqkv[there, 1024 + m * 128 : 1152 + m * 128] = nn(left, right).astype(BF)
    dqkv[:, :512] = dq_flat[...].T
    for part in range(3):
        products(part, dqkv[:, part * 512 : part * 512 + 512])
    pushed = nt(dqkv[...], w_ref[:, :1536])
    both = pushed * unit
    out = dh_ref[...] + scale * (pushed - unit * jnp.mean(both, axis=-1, keepdims=True))
    bg_ref[...] = out
    row_ref[...] = out.astype(BF)
    gains = jnp.concatenate(
        [jnp.sum(both, axis=0, keepdims=True), gain_in[0:1, :], jnp.zeros((14, out.shape[1]), F32)], axis=0
    )
    width, group = out.shape[1], 2 * rows
    gains = pltpu.roll(gains, lax.rem(width - z * group, width), 1)
    lane = lax.broadcasted_iota(jnp.int32, gains.shape, 1)
    swapped = jnp.where(lax.rem(lane, group) < rows, pltpu.roll(gains, width - rows, 1), pltpu.roll(gains, rows, 1))
    here, there = jnp.where(x == 0, gains, swapped), jnp.where(x == 0, swapped, gains)
    for targets, value in (((near_own, near_sib), here), ((far_own, far_sib), there)):
        for target in targets:
            for y in range(2):
                target[y, near.shape[0] :, :] = value.astype(BF)


def column(row):
    n = row.shape[1]
    here = lax.broadcasted_iota(jnp.int32, (n, n), 0) == lax.broadcasted_iota(jnp.int32, (n, n), 1)
    return jnp.sum(jnp.where(here, row, jnp.zeros_like(row)), axis=1, keepdims=True)


def gain_column(gain, k):
    return column(gain[k : k + 1, :].astype(BF).astype(F32))


def adam(master, moment, second, gradient, rate, decay):
    moment_new = 0.5 * moment + 0.5 * gradient
    second_new = 0.6 * second + 0.4 * gradient * gradient
    update = moment_new / (1.0 - 0.5**STEP) / (jnp.sqrt(second_new / (1.0 - 0.6**STEP)) + 1e-08)
    return master - rate * (update + decay * master), moment_new, second_new


def adam_into(outs, state, gradient, rate, decay):
    master, moment, second = adam(*state, gradient, rate, decay)
    outs[0][...] = master
    outs[1][...] = moment
    outs[2][...] = second
    outs[3][...] = master.astype(BF)


def total(refs):
    whole = refs[0][...].astype(F32)
    for ref in refs[1:]:
        whole = whole + ref[...].astype(F32)
    return whole


def feed_update_kernel(count, place_ref, *refs):
    terms_e, terms_s, refs = refs[:count], refs[count : 2 * count], refs[2 * count :]
    gain, state, outs = refs[0], refs[1:7], refs[7:]
    scaled = total(terms_e) * gain_column(gain, 1)
    adam_into(outs[:4], [r[...] for r in state[:3]], scaled, 0.05, 0.1)
    adam_into(outs[4:], [r[...] for r in state[3:]], total(terms_s), 0.025, 0.1)


def attention_update_kernel(count, place_ref, *refs):
    terms, state, outs = refs[:count], refs[count : count + 9], refs[count + 9 :]
    whole = total(terms)
    gain, size = state[0], state[0].shape[1]
    grad = whole[:size]
    gains = []
    for k in range(2):
        at = size + k
        parts = [ref[at : at + 1, 2 * size * n : 2 * size * n + size].astype(F32) for n, ref in enumerate(terms)]
        gains.append(sum(parts[1:], parts[0]))
    gains = jnp.concatenate(gains, axis=0) / gain[...].astype(BF).astype(F32)
    adam_into(outs[8:], [r[...] for r in state[:3]], gains, 0.25, 0.0)
    scale = gain_column(gain, 0)
    state = state[3:]
    for part in range(3):
        master, moment, second = adam(
            *[r[part] for r in state[:3]], grad[:, part * 128 : part * 128 + 128] * scale, 0.05, 0.1
        )
        outs[0][part] = master
        outs[1][part] = moment
        outs[2][part] = second
        outs[3][part] = master.astype(BF)
    adam_into(outs[4:8], [r[...] for r in state[3:]], grad[:, 384:512], 0.3, 0.1)


def prepare_kernel(place_ref, *refs):
    whole, first, second, x_row, c_row = refs[7:12]
    local, sems = refs[12:17], refs[17]
    rows = [pltpu.make_async_copy(refs[5 + k].at[place_ref[2]], (x_row, c_row)[k], sems.at[5 + k]) for k in range(2)]
    copies = [pltpu.make_async_copy(refs[k], local[k], sems.at[k]) for k in range(5)]
    for copy in copies + rows:
        copy.start()
    for copy in copies:
        copy.wait()
    gain, attend, mixing, expand, shrink = local
    gain_one = gain_column(gain, 0)
    gain_two = gain_column(gain, 1)
    cols = expand.shape[1]
    for part in range(3):
        first[:, part * 128 : part * 128 + 128] = (attend[part].astype(BF).astype(F32) * gain_one).astype(BF)
    first[:, 384:512] = mixing[...].astype(BF)
    second[:, :cols] = (expand[...].astype(BF).astype(F32) * gain_two).astype(BF)
    second[:, cols:] = shrink[...].astype(BF)
    whole[:, :512] = first[...]
    whole[:, 512:] = second[...]
    for copy in rows:
        copy.wait()


def put_kernel(messages, place_ref, *refs):
    step = pl.program_id(0)
    for k, ref in enumerate(refs[-1 - messages : -1]):

        @pl.when(step == k)
        def _(ref=ref):
            refs[-1][0] = ref[...].astype(refs[-1].dtype)


def struct(shape, dtype):
    return jax.ShapeDtypeStruct(shape, dtype)


def over_x(value):
    n = lax.axis_size("dp")
    return lax.ppermute(value, "dp", [(i, i ^ 1) for i in range(n)])


def over_z(value, k):
    n = lax.axis_size("dp")
    return lax.ppermute(value, "dp", [(i, (i + 2 * k) % n) for i in range(n)])


def over_y(value):
    return lax.ppermute(value, "mp", [(i, i ^ 2) for i in range(4)])


def over_core(value):
    return lax.ppermute(value, "mp", [(i, i ^ 1) for i in range(4)])


def two_ways(value, first, second):
    n = lax.axis_size("dp")
    pairs = [(dp * 4 + mp, (first, second)[mp % 2](dp, mp)) for dp in range(n) for mp in range(4)]
    return lax.ppermute(value, ("dp", "mp"), [(source, dp * 4 + mp) for source, (dp, mp) in pairs])


def gather_column(block, sibling, count):
    n = 2 * count
    chip = jnp.concatenate([block, sibling], axis=0)
    got = [over_z(block, count // 2)]
    for k in range(1, count // 2):
        got.append(two_ways(chip, lambda d, m, k=k: ((d + 2 * k) % n, m), lambda d, m, k=k: ((d - 2 * k) % n, m)))
    got = jnp.concatenate(got, axis=0)
    return jnp.concatenate([chip, got, over_core(got)], axis=0)


def gather_near(column):
    return two_ways(column, lambda d, m: (d ^ 1, m), lambda d, m: (d, m ^ 2))


def gather_far(near, core):
    half = near.shape[1] // 2
    part = lax.dynamic_slice_in_dim(near, core * half, half, 1)
    return two_ways(part, lambda d, m: (d, m ^ 2), lambda d, m: (d ^ 1, m))


def after(values, *others):
    return lax.optimization_barrier((values, others))[0]


def add(*terms):
    whole = terms[0].astype(F32)
    for term in terms[1:]:
        whole = whole + term.astype(F32)
    return whole.astype(BF)


def scatter_start(grads):
    return add(grads[1], over_core(grads[3]))


def scatter_next(grads, far):
    near, got = grads[0], over_core(grads[2])
    return add(near[0], got[0], far[0]), add(near[1], got[1], far[1])


def put(array, messages, offset, where):
    size = (messages[0].shape[0] // TILE * TILE, messages[0].shape[1])
    kept = [] if offset == 0 else [array]
    return pl.pallas_call(
        functools.partial(put_kernel, len(messages)),
        out_shape=struct((4,) + size, array if offset == 0 else array.dtype),
        grid_spec=pltpu.PrefetchScalarGridSpec(
            num_scalar_prefetch=1,
            grid=(len(messages),),
            in_specs=[pl.BlockSpec(memory_space=pl.ANY)] * len(kept)
            + [pl.BlockSpec(size, lambda i, s: (0, 0))] * len(messages),
            out_specs=pl.BlockSpec((1,) + size, lambda i, s: (s[2] ^ (offset + i), 0, 0)),
        ),
        input_output_aliases={1: 0} if kept else {},
        compiler_params=pltpu.CompilerParams(vmem_limit_bytes=16 * 1024 * 1024),
        cost_estimate=pl.CostEstimate(flops=0, bytes_accessed=16 * messages[0].size, transcendentals=0),
    )(where, *kept, *messages)


def on_device(
    blocks,
    block_segment,
    upstream,
    attend_master,
    attend_first,
    attend_second,
    mixing_master,
    mixing_first,
    mixing_second,
    expand_master,
    expand_first,
    expand_second,
    shrink_master,
    shrink_first,
    shrink_second,
    gains_master,
    gains_first,
    gains_second,
):
    dp_size = lax.axis_size("dp")
    count = dp_size // 2
    rows = attend_master.shape[1]
    length, width = blocks.shape[1:]
    cols = expand_master.shape[1]
    dp_at, mp_at = lax.axis_index("dp"), lax.axis_index("mp")
    where = jnp.stack([dp_at // 2, dp_at % 2, mp_at]).astype(jnp.int32)

    masters = [gains_master, attend_master, mixing_master.T, expand_master, shrink_master.T]
    whole, first, second, x_row, c_row = call(
        prepare_kernel,
        [struct((rows, 512 + 2 * cols), BF), struct((rows, 512), BF), struct((rows, 2 * cols), BF)]
        + [struct((length, width), BF)] * 2,
        masters + [blocks, upstream],
        where,
        scratch=[pltpu.VMEM(a.shape, F32) for a in masters] + [pltpu.SemaphoreType.DMA((7,))],
        outside=range(7),

        limit=60,
        moved=2 << 20,
    )
    core = mp_at % 2
    sibling = over_core(whole)
    column_one = gather_column(first, sibling[:, :512], count)
    column_two = gather_column(second, sibling[:, 512:], count)
    near_one = gather_near(column_one)
    near_two = gather_near(after(column_two, near_one))
    far_one = gather_far(near_one, core)
    sib_far_one = over_core(far_one)
    tiles = length // TILE
    half = count * rows
    h, q, k, v, o, probs, weights = call(
        functools.partial(attention_kernel, count, rows),
        [
            struct((length, width), F32),
            *[struct((length, 512), BF)] * 4,
            struct((8, tiles, 3 * TILE, TILE), BF),
            struct((width, 2048), BF),
        ],
        [x_row, block_segment, column_one, near_one, over_core(near_one), far_one, sib_far_one],
        where,
        scratch=[pltpu.VMEM((512, length), BF)] * 2,
        flops=6 * 10**9,
        moved=12 << 20,
        trans=10**6,
    )
    far_two = gather_far(near_two, core)
    sib_far_two = over_core(after(far_two, h))
    pair = struct((2, 2, half, cols), BF)
    *far_grads, g, dz, w_feed, u_near, c_near, row = call(
        functools.partial(feed_kernel, count, rows),
        [
            *[struct((2, half, cols), BF)] * 4,
            *[struct((length, 4 * cols), BF)] * 2,
            struct((width, 8 * cols), BF),
            *[struct((half, length), BF)] * 2,
            struct((length, width), BF),
        ],
        [h, c_row, column_two, near_two, over_core(near_two), far_two, sib_far_two],
        where,
        scratch=[*[pltpu.VMEM((width, length), BF)] * 2, *[pltpu.VMEM((half, length), BF)] * 2],
        flops=4 * 10**9,
        moved=12 << 20,
        trans=10**6,
    )
    send_x = [add(far_grads[k], over_core(far_grads[k + 1])) for k in (0, 2)]
    g = after(g, send_x)
    near_own, near_sib, dh, gain_two = call(
        feed_rest_kernel,
        [
            pair,
            pair,
            struct((length, width), F32),
            struct((8, width), F32),
        ],
        [h, g, dz, w_feed, u_near, c_near, c_row],
        where,
        flops=4 * 10**9,
        moved=12 << 20,
    )
    far = [over_x(value) for value in send_x]
    row_sib, row_across = over_core(row), over_y(row)
    one = struct((2, half + 16, 512), BF)
    bg, row_low, *grads_one = call(
        functools.partial(attention_back_kernel, count, rows),
        [struct((length, width), F32), struct((length, width), BF), one, one, one, one],
        [x_row, dh, q, k, v, o, probs, weights, gain_two],
        where,
        scratch=[
            *[pltpu.VMEM((width, length), BF)] * 2,
            *[pltpu.VMEM((half, length), BF)] * 2,
            pltpu.VMEM((length, 512), BF),
            *[pltpu.VMEM((512, length), BF)] * 2,
            pltpu.VMEM((2, tiles, 3 * TILE, TILE), BF),
            pltpu.VMEM((length, 1536), BF),
        ],
        flops=8 * 10**9,
        moved=12 << 20,
    )
    bg, row_low = after((bg, row_low), row_across)
    low_sib, low_across = over_core(row_low), over_y(row_low)
    grads_one = after(grads_one, far[1])
    result = put(BF, [row, row_sib, row_across, over_core(row_across)], 0, where)
    send_one = scatter_start(grads_one)
    far_one = over_x(send_one)
    low_far = over_core(after(low_across, far_one))
    blocks_grad = put(F32, [bg, low_sib, low_across, low_far], 0, where)

    got = over_core(near_sib)
    kept_one, send_one_y = scatter_next(grads_one, far_one)
    sums = []
    for k in (1, 0):
        kept, send = [add(near_own[k, y], got[k, y], far[k][y]) for y in range(2)]
        if k == 0:
            send = after(send, low_across)
        sums.append(add(kept, over_y(send)))
    sums = sums[::-1]
    sums[0] = after(sums[0], result)
    terms_two = []
    for value in sums:
        terms_two += [value[:rows]] + [over_z(value[k * rows : (k + 1) * rows], k) for k in range(1, count)]
    sum_one = add(kept_one, over_y(send_one_y))
    parts = [jnp.concatenate([sum_one[k * rows : (k + 1) * rows], sum_one[half:]], axis=0) for k in range(count)]
    terms_one = [over_z(part, k) if k else part for k, part in enumerate(parts)]

    def quad(shape):
        return [struct(shape, F32)] * 3 + [struct(shape, BF)]

    feed_new = call(
        functools.partial(feed_update_kernel, count),
        quad((rows, cols)) * 2,
        [
            *after(terms_two, blocks_grad),
            gains_master,
            expand_master,
            expand_first,
            expand_second,
            shrink_master.T,
            shrink_first.T,
            shrink_second.T,
        ],
        where,
        moved=3 << 20,
    )
    terms_one = after(terms_one, feed_new[0], blocks_grad)
    attention_new = call(
        functools.partial(attention_update_kernel, count),
        quad(attend_master.shape) + quad((rows, 128)) + quad((2, rows)),
        [
            *terms_one,
            gains_master,
            gains_first,
            gains_second,
            attend_master,
            attend_first,
            attend_second,
            mixing_master.T,
            mixing_first.T,
            mixing_second.T,
        ],
        where,
        moved=3 << 20,
    )
    return (
        result,
        blocks_grad,
        *attention_new[:4],
        *[a.T for a in attention_new[4:8]],
        *feed_new[:4],
        *[a.T for a in feed_new[4:]],
        *attention_new[8:],
    )


def solution(mesh):
    rows = P("dp", None, None)
    attend, mixing, expand, gains = P(None, "dp", "mp"), P("mp", "dp"), P("dp", "mp"), P(None, "dp")
    kinds = (attend, mixing, expand, mixing, gains)
    in_specs = (rows, P("dp", None), rows) + tuple(k for k in kinds for _ in range(3))
    out_specs = (rows, rows) + tuple(k for k in kinds for _ in range(4))
    return jax.shard_map(on_device, mesh=mesh, in_specs=in_specs, out_specs=out_specs, check_vma=False)
```
